32 devices in a mesh: dp: 2 (over x), ctx: 8 (over z, y), tensor: 2 (over core).
Axes of the slice: x: 2, y: 2, z: 4, core: 2. Of those that a mesh axis runs over, the one named last changes fastest.
Arguments:
- input_spikes: int32 [512, 4096], P(None, ('dp', 'ctx')), may hold values from 0 to 65535
- query_spikes: int32 [512, 4096], P('tensor', ('dp', 'ctx')), may hold values from 0 to 65535
- key_spikes: int32 [512, 4096], P('tensor', ('dp', 'ctx')), may hold values from 0 to 65535
- values: bfloat16 [4096, 8192], P(('dp', 'ctx'), 'tensor'), may hold values from -6 to 6
- query_slope: bfloat16 [4096, 8192], P(('dp', 'ctx'), 'tensor'), may hold values from 0.25 to 2
- key_slope: bfloat16 [4096, 8192], P(('dp', 'ctx'), 'tensor'), may hold values from 0.25 to 2
- grad_out: bfloat16 [4096, 8192], P(('dp', 'ctx'), 'tensor'), may hold values from -6 to 6
- log_gate: float32 [64, 4096], P('tensor', ('dp', 'ctx')), may hold values from -0.8 to 0
- pattern: int32 [128, 16], P('tensor'), may hold values from 0 to 127, all different within a row
Outputs:
- query_grad: bfloat16 [4096, 8192], P(('dp', 'ctx'), 'tensor')
- key_grad: bfloat16 [4096, 8192], P(('dp', 'ctx'), 'tensor')
- value_grad: float32 [16, 128, 4096], P('ctx', 'tensor')
The draws below stay inside these ranges and needn't reach their ends.
Inputs may be any that keep to these rules, and one draw needn't show every extreme that they name: `pattern`: each column block names 16 different row blocks.
All inputs are finite; a program needn't handle non-finite values.
Results may differ from the reference program's by a relative error of at most 0.0073.
Values sent between devices are 32-bit elements; how exact they have to be, the bound alone decides.
No kernel may reach another device: no remote copies, remote signals or barrier semaphores. Data moves between devices by JAX's collectives and lax.ppermute only.
A program may use at most 192 MiB of HBM per device.

```python
import math
import jax
import jax.numpy as jnp
from jax import lax

D = 8192
ATTENTION_PLANES = 64
HEAD = 128
BLK = 64
TOK_DEV = 256
HE = 8192
NRB = 128
NCB = 128
SEL = 16
SPAN_PER_SERIES = 2048
ALL_ITEMS = 4096


def log_uniform(key, shape, lower_end, upper_end):
    spread = jax.random.uniform(key, shape, jnp.float32)
    return jnp.exp(jnp.log(lower_end) + spread * (jnp.log(upper_end) - jnp.log(lower_end)))


def draw_log_gate(key, part):
    whole_lookup_vectors = jax.random.split(key, 7)
    fast_share = 0.5
    is_fast = jax.random.uniform(whole_lookup_vectors[0], (ATTENTION_PLANES,), jnp.float32) < fast_share
    slow_rate = log_uniform(whole_lookup_vectors[1], (ATTENTION_PLANES,), 0.05, 0.5) / SPAN_PER_SERIES
    fast_rate = log_uniform(whole_lookup_vectors[2], (ATTENTION_PLANES,), 1.0 / 50.0, 1.0 / 30.0)
    head_rate = jnp.where(is_fast, fast_rate, slow_rate)
    block_factor = log_uniform(whole_lookup_vectors[3], (ALL_ITEMS // TOK_DEV,), 0.5, 2.0)
    token_factor = log_uniform(whole_lookup_vectors[4], (ATTENTION_PLANES, ALL_ITEMS), 0.7, 1.4)
    item_indices = jnp.arange(ALL_ITEMS, dtype=jnp.int32)
    block_scale = jnp.take(block_factor, item_indices // TOK_DEV)
    stable_phase_flag = -head_rate[:, None] * block_scale[None, :] * token_factor
    series_number = ALL_ITEMS // SPAN_PER_SERIES
    spike_run_start = jax.random.randint(whole_lookup_vectors[5], (ATTENTION_PLANES, series_number, 2), 0, SPAN_PER_SERIES)
    spike_run_start = spike_run_start + (jnp.arange(series_number, dtype=jnp.int32) * SPAN_PER_SERIES)[None, :, None]
    spike_run_filter = jnp.any(item_indices[None, None, None, :] == spike_run_start[:, :, :, None], axis=(1, 2))
    spike_run_width = jax.random.uniform(whole_lookup_vectors[6], (ATTENTION_PLANES, ALL_ITEMS), jnp.float32, 0.22, 0.69)
    return stable_phase_flag - jnp.where(spike_run_filter, spike_run_width, 0.0)


def plant(entries, stream_key, smallest, largest):
    longest = entries.shape.index(max(entries.shape))
    spots = []
    for shift in (0, 1):
        where = [jax.random.randint(jax.random.fold_in(stream_key, axis), (), 0, length) for axis, length in enumerate(entries.shape)]
        where[longest] = (where[longest] + shift) % entries.shape[longest]
        spots.append(tuple(where))
    return entries.at[spots[0]].set(smallest).at[spots[1]].set(largest)


def level_of(key, dims, cuts, least, top_value):
    def one(axis_at, parts):
        draws = jax.random.uniform(jax.random.fold_in(jax.random.fold_in(key, 6), axis_at), (parts,), jnp.float32, least / len(cuts), top_value / len(cuts))
        return jnp.repeat(jnp.exp(draws), dims[axis_at] // parts).reshape((-1,) + (1,) * (len(dims) - axis_at - 1))

    loudness = one(*cuts[0])
    for cut in cuts[1:]:
        loudness = loudness * one(*cut)
    return loudness


def distinct(own_key, rows, amount, top, lift):
    sequence = jax.random.permutation(jax.random.fold_in(own_key, 1), amount)
    pull = sequence
    for power in range(3):
        pull = pull * pull // amount
    pull = pull * lift // amount
    tickets = jax.random.randint(jax.random.fold_in(own_key, 2), (rows, amount), 0, 4096) + pull
    fixed_rows = jax.random.permutation(jax.random.fold_in(own_key, 3), rows)[jnp.arange(amount) % rows]
    tickets = jnp.where(jnp.arange(rows)[:, None] == fixed_rows[None, :], 1 << 14, tickets)
    merit = tickets * amount + jnp.arange(amount)
    return lax.top_k(merit.astype(jnp.int32), top)[1].astype(jnp.int32)


def noise(own_key, dims, scale, reach, pieces=(), kind=jnp.bfloat16):
    drawn = jax.random.normal(own_key, dims, jnp.float32) * scale
    if len(pieces) > 0:
        drawn = level_of(own_key, dims, pieces, -0.22, 0.18) * drawn
    return jnp.clip(drawn, min=-reach, max=reach).astype(kind)


def setup_inputs(seed: int = 0) -> dict:
    arg_keys = jax.random.split(jax.random.key(seed), 10)
    return {
        "input_spikes": plant(jax.random.randint(arg_keys[0], (D // 16, ALL_ITEMS), 0, 65536), jax.random.fold_in(arg_keys[0], 1), 0, 65535).astype(jnp.int32),
        "query_spikes": plant(jax.random.randint(arg_keys[1], (HE // 16, ALL_ITEMS), 0, 65536), jax.random.fold_in(arg_keys[1], 1), 0, 65535).astype(jnp.int32),
        "key_spikes": plant(jax.random.randint(arg_keys[2], (HE // 16, ALL_ITEMS), 0, 65536), jax.random.fold_in(arg_keys[2], 1), 0, 65535).astype(jnp.int32),
        "values": noise(arg_keys[3], (ALL_ITEMS, HE), 1.0, 6.0, ((0, 16), (1, 2))),
        "query_slope": jnp.clip(jnp.exp(math.log(2.0) - 2.0794415 * jax.random.uniform(arg_keys[4], (ALL_ITEMS, HE), jnp.float32) ** level_of(arg_keys[4], (ALL_ITEMS, HE), ((0, 16), (1, 2)), -0.2, 0.2)), 0.25, 2.0).astype(jnp.bfloat16),
        "key_slope": jnp.clip(jnp.exp(math.log(2.0) - 2.0794415 * jax.random.uniform(arg_keys[5], (ALL_ITEMS, HE), jnp.float32) ** level_of(arg_keys[5], (ALL_ITEMS, HE), ((0, 16), (1, 2)), -0.2, 0.2)), 0.25, 2.0).astype(jnp.bfloat16),
        "grad_out": noise(arg_keys[6], (ALL_ITEMS, HE), 1.0, 6.0, ((0, 16), (1, 2))),
        "log_gate": draw_log_gate(jax.random.fold_in(arg_keys[9], 71), 0),
        "pattern": distinct(arg_keys[8], NCB, NRB, SEL, 0),
    }


highest = lax.Precision.HIGHEST

def dims_of(left_dim, right_dim):
    return (((left_dim,), (right_dim,)), ((), ()))

def unpack_flags(packed):
    shifts = jnp.arange(16, dtype=jnp.int32)
    flags = jnp.bitwise_and(jnp.right_shift(packed[:, None, :], shifts[None, :, None]), 1)
    return flags.reshape(packed.shape[0] * 16, packed.shape[1]).astype(jnp.bfloat16)

def decay_matrix(cumulative):
    spread = cumulative[:, None] - cumulative[None, :]
    places = jnp.arange(cumulative.shape[0])
    causal = places[:, None] >= places[None, :]
    return jnp.where(causal, jnp.exp(jnp.minimum(spread, 0.0)), 0.0)

def first_phase(query_cols, key_cols, head_values, cumulative):
    decays = decay_matrix(cumulative)
    intersection = lax.dot_general(query_cols, key_cols, dims_of(0, 0), preferred_element_type=jnp.float32)
    weights = intersection * decays
    weights_low = weights.astype(jnp.bfloat16)
    local_num = jnp.dot(weights_low, head_values, preferred_element_type=jnp.float32)
    local_den = lax.optimization_barrier(jnp.sum(weights, axis=1))
    tail_decay = jnp.exp(cumulative[-1] - cumulative)
    key_float = key_cols.astype(jnp.float32) * tail_decay[None, :]
    state_sum = jnp.dot(key_float, head_values.astype(jnp.float32), precision=highest)
    key_sum = lax.optimization_barrier(jnp.sum(key_float, axis=1))
    return (weights_low, local_num, local_den, jnp.exp(cumulative[-1]), state_sum, key_sum)

def second_phase(query_cols, key_cols, head_values, head_grad, cumulative, weights_low, local_num, local_den, state_in, keys_in):
    decays = decay_matrix(cumulative)
    lead_decay = jnp.exp(cumulative)
    query_float = query_cols.astype(jnp.float32)
    carried_num = lax.dot_general(query_float, state_in, dims_of(0, 0), precision=highest)
    numerator = local_num + lead_decay[:, None] * carried_num
    denominator = 1.0 + local_den + lead_decay * jnp.dot(keys_in, query_float, precision=highest)
    output = numerator / denominator[:, None]
    grad_float = head_grad.astype(jnp.float32)
    scaled = grad_float / denominator[:, None]
    norm_grad = -lax.optimization_barrier(jnp.sum(grad_float * output, axis=1)) / denominator
    scaled_low = scaled.astype(jnp.bfloat16)
    cross_term = lax.dot_general(scaled_low, head_values, dims_of(1, 1), preferred_element_type=jnp.float32)
    mixed_low = ((cross_term + norm_grad[:, None]) * decays).astype(jnp.bfloat16)
    carried_query = lax.dot_general(scaled, state_in, dims_of(1, 1), precision=highest) + norm_grad[:, None] * keys_in[None, :]
    grad_query = lax.dot_general(mixed_low, key_cols, dims_of(1, 1), preferred_element_type=jnp.float32) + lead_decay[:, None] * carried_query
    grad_key = lax.dot_general(mixed_low, query_cols, dims_of(0, 1), preferred_element_type=jnp.float32)
    grad_value = lax.dot_general(weights_low, scaled_low, dims_of(0, 0), preferred_element_type=jnp.float32)
    adjoint_sum = jnp.dot(query_float * lead_decay[None, :], scaled, precision=highest)
    adjoint_vec = jnp.dot(query_float, lead_decay * norm_grad, precision=highest)
    return (grad_query, grad_key, grad_value, adjoint_sum, adjoint_vec)

def third_phase(key_cols, head_values, cumulative, grad_key_local, grad_value_local, adjoint, adjoint_vec):
    tail_decay = jnp.exp(cumulative[-1] - cumulative)[:, None]
    value_float = head_values.astype(jnp.float32)
    key_float = key_cols.astype(jnp.float32)
    grad_key = grad_key_local + tail_decay * (lax.dot_general(value_float, adjoint, dims_of(1, 1), precision=highest) + adjoint_vec[None, :])
    grad_value = grad_value_local + tail_decay * lax.dot_general(key_float, adjoint, dims_of(0, 0), precision=highest)
    return (grad_key, grad_value)

def sequence_grads(query_cols, key_cols, head_values, head_grad, head_gate):
    blocks = SPAN_PER_SERIES // TOK_DEV
    query_blocks = query_cols.reshape(HEAD, blocks, TOK_DEV).transpose(1, 0, 2)
    key_blocks = key_cols.reshape(HEAD, blocks, TOK_DEV).transpose(1, 0, 2)
    value_blocks = head_values.reshape(blocks, TOK_DEV, HEAD)
    grad_blocks = head_grad.reshape(blocks, TOK_DEV, HEAD)
    cumulative = jnp.cumsum(head_gate.reshape(blocks, TOK_DEV), axis=1)
    weights_low, local_num, local_den, totals, state_sum, key_sum = jax.vmap(first_phase)(query_blocks, key_blocks, value_blocks, cumulative)

    def forward_step(carried, block_items):
        state_now, keys_now = carried
        decay_total, state_add, keys_add = block_items
        return ((decay_total * state_now + state_add, decay_total * keys_now + keys_add), (state_now, keys_now))
    start_state = (jnp.zeros((HEAD, HEAD), jnp.float32), jnp.zeros((HEAD,), jnp.float32))
    unused, (state_in, keys_in) = lax.scan(forward_step, start_state, (totals, state_sum, key_sum))
    grad_query, grad_key, grad_value, adjoint_sum, adjoint_vec = jax.vmap(second_phase)(query_blocks, key_blocks, value_blocks, grad_blocks, cumulative, weights_low, local_num, local_den, state_in, keys_in)

    def backward_step(carried, block_items):
        adjoint_now, vector_now = carried
        decay_total, adjoint_add, vector_add = block_items
        return ((adjoint_add + decay_total * adjoint_now, vector_add + decay_total * vector_now), (adjoint_now, vector_now))
    unused_end, (adjoint_in, vector_in) = lax.scan(backward_step, start_state, (totals, adjoint_sum, adjoint_vec), reverse=True)
    grad_key, grad_value = jax.vmap(third_phase)(key_blocks, value_blocks, cumulative, grad_key, grad_value, adjoint_in, vector_in)
    return (grad_query.reshape(SPAN_PER_SERIES, HEAD), grad_key.reshape(SPAN_PER_SERIES, HEAD), grad_value.reshape(SPAN_PER_SERIES, HEAD))

def reference(input_spikes, query_spikes, key_spikes, values, query_slope, key_slope, grad_out, log_gate, pattern):
    word_rows = HEAD // 16

    def one_head(head_index):
        head_start = head_index.astype(jnp.int32)
        query_cols = unpack_flags(lax.dynamic_slice_in_dim(query_spikes, head_start * word_rows, word_rows, 0))
        key_cols = unpack_flags(lax.dynamic_slice_in_dim(key_spikes, head_start * word_rows, word_rows, 0))
        head_values = lax.dynamic_slice_in_dim(values, head_start * HEAD, HEAD, 1)
        head_grad = lax.dynamic_slice_in_dim(grad_out, head_start * HEAD, HEAD, 1)
        head_gate = lax.dynamic_slice_in_dim(log_gate, head_start, 1, 0)[0]
        result_sets = []
        for seq_index in range(ALL_ITEMS // SPAN_PER_SERIES):
            first_token = seq_index * SPAN_PER_SERIES
            last_token = first_token + SPAN_PER_SERIES
            result_sets.append(sequence_grads(query_cols[:, first_token:last_token], key_cols[:, first_token:last_token], head_values[first_token:last_token], head_grad[first_token:last_token], head_gate[first_token:last_token]))
        return tuple((jnp.concatenate([result_set[part_index] for result_set in result_sets], axis=0) for part_index in range(3)))
    grad_query, grad_key, grad_value = lax.map(one_head, jnp.arange(ATTENTION_PLANES, dtype=jnp.int32))
    flat_query = grad_query.transpose(1, 0, 2).reshape(ALL_ITEMS, ATTENTION_PLANES * HEAD)
    flat_key = grad_key.transpose(1, 0, 2).reshape(ALL_ITEMS, ATTENTION_PLANES * HEAD)
    query_grad = (query_slope.astype(jnp.float32) * flat_query).astype(jnp.bfloat16)
    key_grad = (key_slope.astype(jnp.float32) * flat_key).astype(jnp.bfloat16)
    value_low = grad_value.transpose(1, 0, 2).reshape(ALL_ITEMS, ATTENTION_PLANES * HEAD).astype(jnp.bfloat16)
    input_blocks = unpack_flags(input_spikes).reshape(D // BLK, BLK, ALL_ITEMS)

    def column_grad(column):
        chosen = jnp.take(input_blocks, pattern[column], axis=0).astype(jnp.float32)
        block_values = lax.dynamic_slice_in_dim(value_low, column.astype(jnp.int32) * BLK, BLK, 1).astype(jnp.float32)
        return jnp.einsum('sat,tb->sab', chosen, block_values, precision=highest).reshape(SEL, BLK * BLK)
    value_grad = lax.map(column_grad, jnp.arange(ATTENTION_PLANES * HEAD // BLK, dtype=jnp.int32))
    return (query_grad, key_grad, value_grad.transpose(1, 0, 2))
```

```python
import jax
import jax.numpy as jnp
from jax import lax
from jax.experimental import pallas as pl
from jax.experimental.pallas import tpu as pltpu
from jax.sharding import PartitionSpec as P

HEAD = 128
WORDS = HEAD // 16
BLK = 64
HALF = BLK // 2
SEL = 16
QUAD = 4

F32 = jnp.float32
BF16 = jnp.bfloat16
VMEM_LIMIT = 48 * 1024 * 1024


def params():
    return pltpu.CompilerParams(vmem_limit_bytes=VMEM_LIMIT)


def cost(flops, nbytes):
    return pl.CostEstimate(flops=int(flops), bytes_accessed=int(nbytes), transcendentals=0)


def nn(a, b):
    return lax.dot_general(a, b, (((1,), (0,)), ((), ())), preferred_element_type=F32)


def nt(a, b):
    return lax.dot_general(a, b, (((1,), (1,)), ((), ())), preferred_element_type=F32)


def tn(a, b):
    return lax.dot_general(a, b, (((0,), (0,)), ((), ())), preferred_element_type=F32)


def split(a):
    high = a.astype(BF16)
    return high, (a - high.astype(F32)).astype(BF16)


def fold(a):
    return a[:, :HEAD] + a[:, HEAD:]


def unpack(words):
    tokens = words.shape[1]
    spread = jnp.broadcast_to(words[:, None, :], (WORDS, 16, tokens))
    shifts = lax.broadcasted_iota(jnp.int32, (WORDS, 16, tokens), 1)
    bits = jnp.bitwise_and(jnp.right_shift(spread, shifts), 1)
    return bits.reshape(HEAD, tokens).astype(F32)


def causal(shape, token_axis):
    return lax.broadcasted_iota(jnp.int32, shape, token_axis) >= lax.broadcasted_iota(
        jnp.int32, shape, 1 - token_axis
    )


def lanes(i):
    return slice(i * HEAD, (i + 1) * HEAD)


def rows_of(vector):
    high, low = split(vector)
    low2 = (vector - high.astype(F32) - low.astype(F32)).astype(BF16)
    n = vector.shape[1]
    return jnp.concatenate([high, low, low2, jnp.zeros((13, n), BF16)], axis=0)


def key_sums_kernel(heads, kw, cum, out):
    for i in range(heads):
        row = cum[0, i : i + 1, :]
        tail = jnp.exp(row[:, -1:] - row)
        k = unpack(kw[i * WORDS : (i + 1) * WORDS, :]).astype(BF16)
        out[0, i : i + 1, :] = jnp.sum(nt(rows_of(tail), k), axis=0, keepdims=True)


def summary_kernel(heads, qw, kw, v, cum, y_out, wt_out, den_out, qt_out, kt_out):
    tokens = v.shape[0]
    cols = jnp.transpose(cum[0])
    after = causal((tokens, tokens), 1)
    for i in range(heads):
        row = cum[0, i : i + 1, :]
        col = cols[:, i : i + 1]
        q = unpack(qw[i * WORDS : (i + 1) * WORDS, :])
        k = unpack(kw[i * WORDS : (i + 1) * WORDS, :])
        qt = jnp.transpose(q).astype(BF16)
        kt = jnp.transpose(k).astype(BF16)
        q = q.astype(BF16)
        qt_out[:, lanes(i)] = qt
        kt_out[:, lanes(i)] = kt
        tailed = k * jnp.exp(row[:, -1:] - row)
        high, low = split(tailed)
        value = v[:, lanes(i)]
        y_out[i] = nn(high, value) + nn(low, value)
        decay = jnp.where(after, jnp.exp(jnp.minimum(row - col, 0.0)), 0.0)
        w = nn(kt, q) * decay
        wt_out[i] = w.astype(BF16)
        den_out[0, i : i + 1, :] = jnp.sum(w, axis=0, keepdims=True)


def adjoint_kernel(heads, qw, do, cum, den_local, z0, wt, den_out, x_out, dv_out):
    tokens = do.shape[0]
    rows = []
    qs = []
    for i in range(heads):
        row = cum[0, i : i + 1, :]
        q = unpack(qw[i * WORDS : (i + 1) * WORDS, :]).astype(BF16)
        qs.append(q)
        carried = jnp.sum(nn(rows_of(z0[0, i : i + 1, :]), q), axis=0, keepdims=True)
        rows.append(1.0 + den_local[0, i : i + 1, :] + jnp.exp(row) * carried)
    rows = rows + [jnp.ones((1, tokens), F32)] * (8 - heads)
    den = jnp.concatenate(rows, axis=0)
    den_out[0] = den
    inverse = jnp.transpose(1.0 / den)
    leads = jnp.exp(jnp.transpose(cum[0]))
    for i in range(heads):
        g = do[:, lanes(i)].astype(F32) * inverse[:, i : i + 1]
        x_out[i] = fold(nn(qs[i], jnp.concatenate(split(g * leads[:, i : i + 1]), axis=1)))
        dv_out[0, :, lanes(i)] = nn(wt[i], g.astype(BF16))


def value_kernel(heads, c, kt, dv_local, cum, out):
    cols = jnp.transpose(cum[0])
    for i in range(heads):
        col = cols[:, i : i + 1]
        tail = jnp.exp(col[-1:, :] - col)
        carried = fold(nn(kt[:, lanes(i)], jnp.concatenate(split(c[i]), axis=1)))
        dv = dv_local[0, :, lanes(i)] + tail * carried
        out[0, :, lanes(i)] = dv.astype(BF16).astype(F32)


def token_kernel(heads, s0, c, z0, qt, kt, v, do, den, cum, slope, dq_out, dk_out, xv_out):
    tokens = v.shape[0]
    cols = jnp.transpose(cum[0])
    inverses = jnp.transpose(1.0 / den[0])
    before = causal((tokens, tokens), 0)
    for i in range(heads):
        row = cum[0, i : i + 1, :]
        col = cols[:, i : i + 1]
        inverse = inverses[:, i : i + 1]
        lead = jnp.exp(col)
        tail = jnp.exp(col[-1:, :] - col)
        q = qt[:, lanes(i)]
        k = kt[:, lanes(i)]
        value = v[:, lanes(i)]
        grad = do[:, lanes(i)].astype(F32)
        decay = jnp.where(before, jnp.exp(jnp.minimum(col - row, 0.0)), 0.0)
        w = (nt(q, k) * decay).astype(BF16)
        state = split(s0[i])
        carried = fold(nn(q, jnp.concatenate(state, axis=1)))
        o = (nn(w, value) + lead * carried) * inverse
        h = -jnp.sum(grad * o, axis=1, keepdims=True) * inverse
        g = (grad * inverse).astype(BF16)
        r = ((nt(g, value) + h) * decay).astype(BF16)
        back = fold(nt(g, jnp.concatenate(state, axis=0))) + h * z0[0, i : i + 1, :]
        dq = nn(r, k) + lead * back
        dq_out[:, lanes(i)] = (slope[:, lanes(i)].astype(F32) * dq).astype(BF16)
        carried = fold(nt(value, jnp.concatenate(split(c[i]), axis=0)))
        dk_out[:, lanes(i)] = tn(r, q) + tail * carried
        xv_out[0, i : i + 1, :] = jnp.sum(q.astype(F32) * (lead * h), axis=0, keepdims=True)


def key_kernel(heads, dk, cv, cum, slope, out):
    cols = jnp.transpose(cum[0])
    for i in range(heads):
        col = cols[:, i : i + 1]
        tail = jnp.exp(col[-1:, :] - col)
        total = dk[:, lanes(i)] + tail * cv[0, i : i + 1, :]
        out[:, lanes(i)] = (slope[:, lanes(i)].astype(F32) * total).astype(BF16)


def block_kernel(pattern, *refs):
    spikes, grads, out, flags = refs[:QUAD], refs[QUAD : 2 * QUAD], refs[2 * QUAD], refs[2 * QUAD + 1]
    tokens = grads[0].shape[0]
    step = pl.program_id(0)
    shifts = 2 * lax.broadcasted_iota(jnp.int32, (8, tokens), 0)
    low = lax.broadcasted_iota(jnp.int32, (tokens, HEAD), 1) < BLK
    for side in range(2):
        total = None
        for source in range(QUAD):
            grad = grads[source][...]
            turned = jnp.concatenate([grad[:, BLK:], grad[:, :BLK]], axis=1)
            even, odd = (grad, turned) if side == 0 else (turned, grad)
            right = jnp.concatenate(
                [jnp.where(low, even, 0.0).astype(BF16), jnp.where(low, 0.0, odd).astype(BF16)], axis=0
            )
            for s in range(SEL):
                first = pattern[2 * step + side, s] * (BLK // 16)
                for parity in range(2):
                    parts = []
                    for word in range(BLK // 16):
                        line = spikes[source][pl.ds(first + word, 1), :]
                        spread = jnp.broadcast_to(line, (8, tokens))
                        parts.append(jnp.bitwise_and(jnp.right_shift(spread, shifts + parity), 1))
                    bits = jnp.concatenate(parts, axis=0).astype(F32).astype(BF16)
                    flags[s * HALF : (s + 1) * HALF, parity * tokens : (parity + 1) * tokens] = bits
            part = nn(flags[...], right)
            total = part if total is None else total + part
        out[:, side] = total.reshape(SEL, HALF, HEAD)


def per_device(
    input_spikes,
    query_spikes,
    key_spikes,
    values,
    query_slope,
    key_slope,
    grad_out,
    log_gate,
    pattern,
):
    tokens, width = values.shape
    heads_here = width // HEAD
    heads = heads_here // QUAD
    nctx, ndp = lax.axis_size("ctx"), lax.axis_size("dp")
    nz = nctx // 2
    x, place = lax.axis_index("dp"), lax.axis_index("ctx")
    y, z = place % 2, place // 2

    gate_sums = jnp.cumsum(log_gate, axis=1)
    totals = jnp.exp(gate_sums[:, -1])
    cum = gate_sums.reshape(QUAD, heads, tokens)
    cum = jnp.pad(cum, ((0, 0), (0, 8 - heads), (0, 0)))

    word_spec = pl.BlockSpec((heads * WORDS, tokens), lambda j: (j, 0))
    flat_spec = pl.BlockSpec((tokens, heads * HEAD), lambda j: (0, j))
    quad_spec = pl.BlockSpec((1, tokens, heads * HEAD), lambda j: (j, 0, 0))
    cum_spec = pl.BlockSpec((1, 8, tokens), lambda j: (j, 0, 0))
    vec_spec = pl.BlockSpec((1, 8, HEAD), lambda j: (j, 0, 0))
    state_spec = pl.BlockSpec((heads, HEAD, HEAD), lambda j: (j, 0, 0))
    wt_spec = pl.BlockSpec((heads, tokens, tokens), lambda j: (j, 0, 0))

    def shape(*dims, kind=F32):
        return jax.ShapeDtypeStruct(dims, kind)

    flat16 = shape(tokens, width, kind=BF16)
    flat32 = shape(tokens, width)
    quad32 = shape(QUAD, tokens, heads * HEAD)
    states = shape(heads_here, HEAD, HEAD)
    vecs = shape(QUAD, 8, HEAD)
    cums = shape(QUAD, 8, tokens)
    unit = 2 * tokens * tokens * HEAD * heads_here
    mib = 1 << 20

    def call(kernel, in_specs, out_specs, out_shape, estimate, *args):
        def body(*refs):
            kernel(heads, *refs)

        body.__name__ = kernel.__name__
        return pl.pallas_call(
            body,
            grid=(QUAD,),
            in_specs=in_specs,
            out_specs=out_specs,
            out_shape=out_shape,
            compiler_params=params(),
            cost_estimate=estimate,
            name=kernel.__name__,
        )(*args)

    def swap(value, dx, dy):
        pairs = [
            (d * nctx + c, (d ^ dx) * nctx + (c ^ dy)) for d in range(ndp) for c in range(nctx)
        ]
        return lax.ppermute(value, ("dp", "ctx"), pairs)

    def along(value, delta):
        pairs = [
            (c, c + 2 * delta) for c in range(nctx) if 0 <= c + 2 * delta < nctx
        ]
        return lax.ppermute(value, "ctx", pairs)

    def vec(a):
        return jnp.pad(a.reshape(QUAD, heads, HEAD), ((0, 0), (0, 8 - heads), (0, 0)))

    def unvec(a):
        return a[:, :heads].reshape(heads_here, HEAD)

    def everyone(value):
        parts = [value]
        for k in range(1, nctx):
            parts.append(lax.ppermute(value, "ctx", [(c, (c + k) % nctx) for c in range(nctx)]))
        return parts

    key_sum = call(
        key_sums_kernel, [word_spec, cum_spec], vec_spec, vecs, cost(unit // 16, mib), key_spikes, cum
    )
    message = jnp.concatenate(
        [unvec(key_sum), jnp.broadcast_to(totals[:, None], (heads_here, HEAD))], axis=0
    )
    messages = everyone(message)

    state_sum, wt, den_local, qt, kt = call(
        summary_kernel,
        [word_spec, word_spec, flat_spec, cum_spec],
        [state_spec, wt_spec, cum_spec, flat_spec, flat_spec],
        [states, shape(heads_here, tokens, tokens, kind=BF16), cums, flat16, flat16],
        cost(3 * unit, 14 * mib),
        query_spikes,
        key_spikes,
        values,
        cum,
    )

    z0 = jnp.zeros((heads_here, HEAD), F32)
    for k in range(nctx - 1, 0, -1):
        part = messages[k]
        z0 = jnp.where(place >= k, part[heads_here:] * z0 + part[:heads_here], z0)
    z0 = vec(z0)
    relative = jnp.stack([part[heads_here:, 0] for part in messages])
    decays = jnp.take(relative, (place - jnp.arange(nctx)) % nctx, axis=0)
    pair_decays = decays[0::2] * decays[1::2]

    den, adjoint_sum, dv_local = call(
        adjoint_kernel,
        [word_spec, flat_spec, cum_spec, cum_spec, vec_spec, wt_spec],
        [cum_spec, state_spec, quad_spec],
        [cums, states, quad32],
        cost(3 * unit, 14 * mib),
        query_spikes,
        grad_out,
        cum,
        den_local,
        z0,
        wt,
    )

    half = heads_here // 2
    mine, other = y * half, (1 - y) * half

    def cut(value, start):
        return lax.dynamic_slice_in_dim(value, start, half, 0)

    def decay_at(at):
        row = lax.dynamic_index_in_dim(pair_decays, jnp.clip(at, 0, nz - 1), 0, keepdims=False)
        return cut(row, mine)[:, None, None]

    first_decay = cut(lax.dynamic_index_in_dim(decays, 2 * z, 0, keepdims=False), mine)[:, None, None]
    second_decay = cut(lax.dynamic_index_in_dim(decays, 2 * z + 1, 0, keepdims=False), mine)[:, None, None]

    def carried(value, forward):
        own = cut(value, mine)
        got = swap(cut(value, other), 0, 1)
        first = jnp.where(y == 0, own, got)
        second = jnp.where(y == 0, got, own)
        both = second_decay * first + second if forward else first + first_decay * second
        sign = 1 if forward else -1
        arrived = [along(both, sign * delta) for delta in range(1, nz)]
        reach = arrived[-1]
        for delta in range(nz - 2, 0, -1):
            reach = decay_at(z - sign * delta) * reach + arrived[delta - 1]
        if forward:
            for_first, for_second = reach, first_decay * reach + first
        else:
            for_first, for_second = second + second_decay * reach, reach
        keep = jnp.where(y == 0, for_first, for_second)
        got = swap(jnp.where(y == 0, for_second, for_first), 0, 1)
        return jnp.concatenate([jnp.where(y == 0, keep, got), jnp.where(y == 0, got, keep)], axis=0)

    adjoint = carried(adjoint_sum, False)
    state = carried(state_sum, True)

    value_low = call(
        value_kernel,
        [state_spec, flat_spec, quad_spec, cum_spec],
        quad_spec,
        quad32,
        cost(unit // 2, 12 * mib),
        adjoint,
        kt,
        dv_local,
        cum,
    )

    quad = 2 * x + y
    offsets = [(0, 0), (0, 1), (1, 0), (1, 1)]

    def quarter(dx, dy):
        part = lax.dynamic_index_in_dim(value_low, 2 * (x ^ dx) + (y ^ dy), 0, keepdims=False)
        return part if (dx, dy) == (0, 0) else swap(part, dx, dy)

    grads = [quarter(*offset) for offset in offsets]
    spikes = [input_spikes] + [swap(input_spikes, *offset) for offset in offsets[1:]]

    dq, dk, xv = call(
        token_kernel,
        [state_spec, state_spec, vec_spec] + [flat_spec] * 4 + [cum_spec, cum_spec, flat_spec],
        [flat_spec, flat_spec, vec_spec],
        [flat16, flat32, vecs],
        cost(6 * unit, 20 * mib),
        state,
        adjoint,
        z0,
        qt,
        kt,
        values,
        grad_out,
        den,
        cum,
        query_slope,
    )
    vectors = everyone(unvec(xv))
    cv = jnp.zeros((heads_here, HEAD), F32)
    for k in range(nctx - 1, 0, -1):
        part = vectors[nctx - k]
        at = jnp.clip(place + k, 0, nctx - 1)
        decay = lax.dynamic_index_in_dim(decays, at, 0, keepdims=False)[:, None]
        cv = jnp.where(place + k < nctx, part + decay * cv, cv)
    key_grad = call(
        key_kernel,
        [flat_spec, vec_spec, cum_spec, flat_spec],
        flat_spec,
        flat16,
        cost(1, 8 * mib),
        dk,
        vec(cv),
        cum,
        key_slope,
    )

    columns = pattern.shape[0] // QUAD
    own_pattern = lax.dynamic_slice_in_dim(pattern, quad * columns, columns, 0)
    partial_value = pl.pallas_call(
        block_kernel,
        grid_spec=pltpu.PrefetchScalarGridSpec(
            num_scalar_prefetch=1,
            grid=(columns // 2,),
            in_specs=[pl.BlockSpec(input_spikes.shape, lambda j, p: (0, 0))] * QUAD
            + [pl.BlockSpec((tokens, HEAD), lambda j, p: (0, j))] * QUAD,
            out_specs=pl.BlockSpec((SEL, 2, HALF, HEAD), lambda j, p: (0, j, 0, 0)),
            scratch_shapes=[pltpu.VMEM((SEL * HALF, 2 * tokens), BF16)],
        ),
        out_shape=shape(SEL, columns, HALF, HEAD),
        compiler_params=params(),
        cost_estimate=cost(2 * unit, 10 * mib),
        name="block_kernel",
    )(own_pattern, *spikes, *grads)

    share = SEL // nz
    pieces = partial_value.reshape(nz, share, columns, HALF, HEAD)

    def piece(at):
        return lax.dynamic_index_in_dim(pieces, jnp.clip(at, 0, nz - 1), 0, keepdims=False)

    up = down = None
    for step in range(nz - 1):
        send_up = piece(nz - 1 - step + z)
        send_down = piece(step - (nz - 1 - z))
        if step:
            send_up, send_down = send_up + up, send_down + down
        up = lax.ppermute(
            send_up, "ctx", [(c, c + 2) for c in range(nctx - 2) if c // 2 <= step]
        )
        down = lax.ppermute(
            send_down, "ctx", [(c, c - 2) for c in range(2, nctx) if nz - 1 - c // 2 <= step]
        )
    summed = piece(z) + up + down

    def rows(dx, dy):
        part = lax.dynamic_slice_in_dim(summed, (y ^ dy) * (share // 2), share // 2, 0)
        return part if (dx, dy) == (0, 0) else swap(part, dx, dy)

    parts = [rows(*offset) for offset in offsets]
    parts = [jnp.where(y == 0, parts[i], parts[i ^ 1]) for i in range(QUAD)]
    parts = [jnp.where(x == 0, parts[i], parts[i ^ 2]) for i in range(QUAD)]
    value_grad = jnp.concatenate(parts, axis=1).reshape(share // 2, QUAD * columns, BLK * BLK)
    return (dq, key_grad, value_grad)


def solution(mesh):
    in_specs = (
        P(None, ("dp", "ctx")),
        P("tensor", ("dp", "ctx")),
        P("tensor", ("dp", "ctx")),
        P(("dp", "ctx"), "tensor"),
        P(("dp", "ctx"), "tensor"),
        P(("dp", "ctx"), "tensor"),
        P(("dp", "ctx"), "tensor"),
        P("tensor", ("dp", "ctx")),
        P("tensor", None),
    )
    out_specs = (P(("dp", "ctx"), "tensor"), P(("dp", "ctx"), "tensor"), P("ctx", "tensor", None))
    return jax.shard_map(
        per_device, mesh=mesh, in_specs=in_specs, out_specs=out_specs, check_vma=False
    )
```

```python
import jax
import jax.numpy as jnp
from jax import lax
from jax.experimental import pallas as pl
from jax.experimental.pallas import tpu as pltpu
from jax.sharding import PartitionSpec as P

HEAD = 128
WORDS = HEAD // 16
BLK = 64
HALF = BLK // 2
SEL = 16
QUAD = 4
CHUNKS = 2

F32 = jnp.float32
BF16 = jnp.bfloat16
VMEM_LIMIT = 48 * 1024 * 1024


def params():
    return pltpu.CompilerParams(vmem_limit_bytes=VMEM_LIMIT)


def cost(flops, nbytes):
    return pl.CostEstimate(flops=int(flops), bytes_accessed=int(nbytes), transcendentals=0)


def nn(a, b):
    return lax.dot_general(a, b, (((1,), (0,)), ((), ())), preferred_element_type=F32)


def nt(a, b):
    return lax.dot_general(a, b, (((1,), (1,)), ((), ())), preferred_element_type=F32)


def tn(a, b):
    return lax.dot_general(a, b, (((0,), (0,)), ((), ())), preferred_element_type=F32)


def split(a):
    high = a.astype(BF16)
    return high, (a - high.astype(F32)).astype(BF16)


def fold(a):
    return a[:, :HEAD] + a[:, HEAD:]


def unpack(words):
    tokens = words.shape[1]
    spread = jnp.broadcast_to(words[:, None, :], (WORDS, 16, tokens))
    shifts = lax.broadcasted_iota(jnp.int32, (WORDS, 16, tokens), 1)
    bits = jnp.bitwise_and(jnp.right_shift(spread, shifts), 1)
    return bits.reshape(HEAD, tokens).astype(F32)


def causal(shape, token_axis):
    return lax.broadcasted_iota(jnp.int32, shape, token_axis) >= lax.broadcasted_iota(
        jnp.int32, shape, 1 - token_axis
    )


def lanes(i):
    return slice(i * HEAD, (i + 1) * HEAD)


def rows_of(vector):
    high, low = split(vector)
    low2 = (vector - high.astype(F32) - low.astype(F32)).astype(BF16)
    n = vector.shape[1]
    return jnp.concatenate([high, low, low2, jnp.zeros((13, n), BF16)], axis=0)


def key_sums_kernel(heads, kw, cum, out):
    for i in range(heads):
        row = cum[0, i : i + 1, :]
        tail = jnp.exp(row[:, -1:] - row)
        k = unpack(kw[i * WORDS : (i + 1) * WORDS, :]).astype(BF16)
        out[0, i : i + 1, :] = jnp.sum(nt(rows_of(tail), k), axis=0, keepdims=True)


def summary_kernel(heads, qw, kw, v, cum, y_out, wt_out, den_out, qt_out, kt_out):
    tokens = v.shape[0]
    cols = jnp.transpose(cum[0])
    after = causal((tokens, tokens), 1)
    for i in range(heads):
        row = cum[0, i : i + 1, :]
        col = cols[:, i : i + 1]
        q = unpack(qw[i * WORDS : (i + 1) * WORDS, :])
        k = unpack(kw[i * WORDS : (i + 1) * WORDS, :])
        qt = jnp.transpose(q).astype(BF16)
        kt = jnp.transpose(k).astype(BF16)
        q = q.astype(BF16)
        qt_out[:, lanes(i)] = qt
        kt_out[:, lanes(i)] = kt
        tailed = k * jnp.exp(row[:, -1:] - row)
        high, low = split(tailed)
        value = v[:, lanes(i)]
        y_out[i] = nn(high, value) + nn(low, value)
        decay = jnp.where(after, jnp.exp(jnp.minimum(row - col, 0.0)), 0.0)
        w = nn(kt, q) * decay
        wt_out[i] = w.astype(BF16)
        den_out[0, i : i + 1, :] = jnp.sum(w, axis=0, keepdims=True)


def adjoint_kernel(start, heads, qw, do, cum, den_local, z0, wt, den_out, x_out, dv_out):
    tokens = do.shape[0]
    rows = []
    qs = []
    for i in range(heads):
        at = start + i
        row = cum[0, at : at + 1, :]
        q = unpack(qw[i * WORDS : (i + 1) * WORDS, :]).astype(BF16)
        qs.append(q)
        carried = jnp.sum(nn(rows_of(z0[0, at : at + 1, :]), q), axis=0, keepdims=True)
        rows.append(1.0 + den_local[0, at : at + 1, :] + jnp.exp(row) * carried)
    rows = rows + [jnp.ones((1, tokens), F32)] * (8 - heads)
    den = jnp.concatenate(rows, axis=0)
    den_out[0] = den
    inverse = jnp.transpose(1.0 / den)
    leads = jnp.exp(jnp.transpose(cum[0]))
    for i in range(heads):
        g = do[:, lanes(i)].astype(F32) * inverse[:, i : i + 1]
        lead = leads[:, start + i : start + i + 1]
        x_out[0, i] = fold(nn(qs[i], jnp.concatenate(split(g * lead), axis=1)))
        dv_out[0, :, lanes(i)] = nn(wt[i], g.astype(BF16))


def output_kernel(chunk, heads, s0, qt, kt, v, do, cum, *refs):
    dens, (h_out, xv_out) = refs[:-2], refs[-2:]
    tokens = v.shape[0]
    cols = jnp.transpose(cum[0])
    inverses = [jnp.transpose(1.0 / den[0]) for den in dens]
    before = causal((tokens, tokens), 0)
    for i in range(heads):
        row = cum[0, i : i + 1, :]
        col = cols[:, i : i + 1]
        inverse = inverses[i // chunk][:, i % chunk : i % chunk + 1]
        lead = jnp.exp(col)
        q = qt[:, lanes(i)]
        grad = do[:, lanes(i)].astype(F32)
        decay = jnp.where(before, jnp.exp(jnp.minimum(col - row, 0.0)), 0.0)
        w = (nt(q, kt[:, lanes(i)]) * decay).astype(BF16)
        carried = fold(nn(q, jnp.concatenate(split(s0[i]), axis=1)))
        o = (nn(w, v[:, lanes(i)]) + lead * carried) * inverse
        h = -jnp.sum(grad * o, axis=1, keepdims=True) * inverse
        h_out[0, :, i : i + 1] = h
        xv_out[0, i : i + 1, :] = jnp.sum(q.astype(F32) * (lead * h), axis=0, keepdims=True)


def token_kernel(chunk, heads, turn, s0, c, z0, qt, kt, v, do, cum, slope, h_in, *refs):
    dens, (dq_out, dk_out) = refs[:-2], refs[-2:]
    tokens = v.shape[0]
    cols = jnp.transpose(cum[0])
    inverses = [jnp.transpose(1.0 / den[0]) for den in dens]
    before = causal((tokens, tokens), 0)
    for i in range(heads):
        row = cum[0, i : i + 1, :]
        col = cols[:, i : i + 1]
        inverse = inverses[i // chunk][:, i % chunk : i % chunk + 1]
        lead = jnp.exp(col)
        tail = jnp.exp(col[-1:, :] - col)
        value = v[:, lanes(i)]
        decay = jnp.where(before, jnp.exp(jnp.minimum(col - row, 0.0)), 0.0)
        h = h_in[0, :, i : i + 1]
        g = (do[:, lanes(i)].astype(F32) * inverse).astype(BF16)
        r = ((nt(g, value) + h) * decay).astype(BF16)
        back = fold(nt(g, jnp.concatenate(split(s0[i]), axis=0))) + h * z0[0, i : i + 1, :]
        dq = nn(r, kt[:, lanes(i)]) + lead * back
        dq_out[:, lanes(i)] = (slope[:, lanes(i)].astype(F32) * dq).astype(BF16)
        carried = fold(nt(value, jnp.concatenate(split(c[0, i]), axis=0)))
        dk_out[:, lanes(i)] = tn(r, qt[:, lanes(i)]) + tail * carried


def key_kernel(heads, dk, cv, cum, slope, out):
    cols = jnp.transpose(cum[0])
    for i in range(heads):
        col = cols[:, i : i + 1]
        tail = jnp.exp(col[-1:, :] - col)
        total = dk[:, lanes(i)] + tail * cv[0, i : i + 1, :]
        out[:, lanes(i)] = (slope[:, lanes(i)].astype(F32) * total).astype(BF16)


def block_kernel(start, pattern, *refs):
    spikes, grads, words, cums, adjoints = (refs[QUAD * i : QUAD * (i + 1)] for i in range(5))
    out, flags = refs[5 * QUAD :]
    tokens = grads[0].shape[0]
    step = pl.program_id(0)
    shifts = 2 * lax.broadcasted_iota(jnp.int32, (8, tokens), 0)
    low = lax.broadcasted_iota(jnp.int32, (tokens, HEAD), 1) < BLK
    values = []
    for source in range(QUAD):
        row = cums[source][pl.ds(start + step, 1), :]
        k = unpack(words[source][...].astype(jnp.int32)) * jnp.exp(row[:, -1:] - row)
        carried = fold(tn(k.astype(BF16), jnp.concatenate(split(adjoints[source][0]), axis=1)))
        values.append((grads[source][...] + carried).astype(BF16).astype(F32))
    for side in range(2):
        total = None
        for source in range(QUAD):
            grad = values[source]
            turned = jnp.concatenate([grad[:, BLK:], grad[:, :BLK]], axis=1)
            even, odd = (grad, turned) if side == 0 else (turned, grad)
            right = jnp.concatenate(
                [jnp.where(low, even, 0.0).astype(BF16), jnp.where(low, 0.0, odd).astype(BF16)], axis=0
            )
            for s in range(SEL):
                first = pattern[2 * (start + step) + side, s] * (BLK // 16)
                for parity in range(2):
                    parts = []
                    for word in range(BLK // 16):
                        line = spikes[source][pl.ds(first + word, 1), :]
                        spread = jnp.broadcast_to(line, (8, tokens))
                        parts.append(jnp.bitwise_and(jnp.right_shift(spread, shifts + parity), 1))
                    bits = jnp.concatenate(parts, axis=0).astype(F32).astype(BF16)
                    flags[s * HALF : (s + 1) * HALF, parity * tokens : (parity + 1) * tokens] = bits
            part = nn(flags[...], right)
            total = part if total is None else total + part
        out[:, side] = total.reshape(SEL, HALF, HEAD)


def per_device(
    input_spikes,
    query_spikes,
    key_spikes,
    values,
    query_slope,
    key_slope,
    grad_out,
    log_gate,
    pattern,
):
    tokens, width = values.shape
    heads_here = width // HEAD
    heads = heads_here // QUAD
    chunk = heads // CHUNKS
    nctx, ndp = lax.axis_size("ctx"), lax.axis_size("dp")
    nz = nctx // 2
    x, place = lax.axis_index("dp"), lax.axis_index("ctx")
    y, z = place % 2, place // 2
    quad = 2 * x + y
    offsets = [(0, 0), (0, 1), (1, 0), (1, 1)]

    gate_sums = jnp.cumsum(log_gate, axis=1)
    totals = jnp.exp(gate_sums[:, -1])
    cum = gate_sums.reshape(QUAD, heads, tokens)
    cum = jnp.pad(cum, ((0, 0), (0, 8 - heads), (0, 0)))

    def spec(block, index):
        return pl.BlockSpec(block, lambda j, *refs: index(j))

    word_spec = spec((heads * WORDS, tokens), lambda j: (j, 0))
    flat_spec = spec((tokens, heads * HEAD), lambda j: (0, j))
    cum_spec = spec((1, 8, tokens), lambda j: (j, 0, 0))
    vec_spec = spec((1, 8, HEAD), lambda j: (j, 0, 0))
    state_spec = spec((heads, HEAD, HEAD), lambda j: (j, 0, 0))
    wt_spec = spec((heads, tokens, tokens), lambda j: (j, 0, 0))
    col_spec = spec((1, tokens, 8), lambda j: (j, 0, 0))

    def shape(*dims, kind=F32):
        return jax.ShapeDtypeStruct(dims, kind)

    flat16 = shape(tokens, width, kind=BF16)
    flat32 = shape(tokens, width)
    states = shape(heads_here, HEAD, HEAD)
    vecs = shape(QUAD, 8, HEAD)
    cums = shape(QUAD, 8, tokens)
    unit = 2 * tokens * tokens * HEAD * heads_here
    mib = 1 << 20

    def call(name, kernel, in_specs, out_specs, out_shape, estimate, *args):
        def body(*refs):
            kernel(*refs)

        body.__name__ = name
        return pl.pallas_call(
            body,
            grid=(QUAD,),
            in_specs=in_specs,
            out_specs=out_specs,
            out_shape=out_shape,
            compiler_params=params(),
            cost_estimate=estimate,
            name=name,
        )(*args)

    def swap(value, dx, dy):
        pairs = [
            (d * nctx + c, (d ^ dx) * nctx + (c ^ dy)) for d in range(ndp) for c in range(nctx)
        ]
        return lax.ppermute(value, ("dp", "ctx"), pairs)

    def along(value, delta, only=None):
        pairs = [
            (c, c + 2 * delta)
            for c in range(nctx)
            if 0 <= c + 2 * delta < nctx and (only is None or c // 2 == only)
        ]
        return lax.ppermute(value, "ctx", pairs)

    def vec(a):
        return jnp.pad(a.reshape(QUAD, heads, HEAD), ((0, 0), (0, 8 - heads), (0, 0)))

    def unvec(a):
        return a[:, :heads].reshape(heads_here, HEAD)

    def ordered(own, got):
        return jnp.where(y == 0, own, got), jnp.where(y == 0, got, own)

    def at_group(value, dx, dy):
        return lax.dynamic_index_in_dim(value, 2 * (x ^ dx) + (y ^ dy), 0, keepdims=False)

    spread_totals = jnp.broadcast_to(totals[:, None], (heads_here, HEAD))

    def carried_vectors(vector, forward):
        message = jnp.concatenate([vector, spread_totals], axis=0)
        first, second = ordered(message, swap(message, 0, 1))
        first_decay, second_decay = first[heads_here:], second[heads_here:]
        first, second = first[:heads_here], second[:heads_here]
        both = second_decay * first + second if forward else first + first_decay * second
        message = jnp.concatenate([both, first_decay * second_decay], axis=0)
        sign = 1 if forward else -1
        arrived = [along(message, sign * delta) for delta in range(1, nz)]
        reach = arrived[-1][:heads_here]
        for part in arrived[-2::-1]:
            reach = part[heads_here:] * reach + part[:heads_here]
        if forward:
            return jnp.where(y == 0, reach, first_decay * reach + first)
        return jnp.where(y == 0, second + second_decay * reach, reach)

    key_sum = call(
        "key_sums_kernel",
        lambda *refs: key_sums_kernel(heads, *refs),
        [word_spec, cum_spec],
        vec_spec,
        vecs,
        cost(unit // 16, mib),
        key_spikes,
        cum,
    )
    z0 = vec(carried_vectors(unvec(key_sum), True))

    state_sum, wt, den_local, qt, kt = call(
        "summary_kernel",
        lambda *refs: summary_kernel(heads, *refs),
        [word_spec, word_spec, flat_spec, cum_spec],
        [state_spec, wt_spec, cum_spec, flat_spec, flat_spec],
        [states, shape(heads_here, tokens, tokens, kind=BF16), cums, flat16, flat16],
        cost(3 * unit, 14 * mib),
        query_spikes,
        key_spikes,
        values,
        cum,
    )

    dens, adjoint_sums, value_parts = [], [], []
    for n in range(CHUNKS):
        den, adjoint_sum, value_part = call(
            "adjoint_kernel",
            lambda *refs, n=n: adjoint_kernel(n * chunk, chunk, *refs),
            [
                spec((chunk * WORDS, tokens), lambda j, n=n: (j * CHUNKS + n, 0)),
                spec((tokens, chunk * HEAD), lambda j, n=n: (0, j * CHUNKS + n)),
                cum_spec,
                cum_spec,
                vec_spec,
                spec((chunk, tokens, tokens), lambda j, n=n: (j * CHUNKS + n, 0, 0)),
            ],
            [
                cum_spec,
                spec((1, chunk, HEAD, HEAD), lambda j: (j, 0, 0, 0)),
                spec((1, tokens, chunk * HEAD), lambda j: (j, 0, 0)),
            ],
            [cums, shape(QUAD, chunk, HEAD, HEAD), shape(QUAD, tokens, chunk * HEAD)],
            cost(3 * unit // CHUNKS, 14 * mib // CHUNKS),
            query_spikes,
            grad_out,
            cum,
            den_local,
            z0,
            wt,
        )
        dens.append(den)
        adjoint_sums.append(adjoint_sum)
        value_parts.append(value_part)

    def plane(value):
        return [at_group(value, 0, 0)] + [
            swap(at_group(value, *offset), *offset) for offset in offsets[1:]
        ]

    key_words = jnp.concatenate(
        [key_spikes.reshape(QUAD, heads * WORDS, tokens).astype(F32), cum], axis=1
    )
    key_words = plane(key_words)
    spikes = [input_spikes] + [swap(input_spikes, *offset) for offset in offsets[1:]]

    def pair_of(parts, dx):
        return ordered(parts[2 * dx], parts[2 * dx + 1])

    adjoints = []
    for n in range(CHUNKS):
        parts = plane(adjoint_sums[n])
        gates = [
            jnp.exp(part[heads * WORDS + n * chunk : heads * WORDS + (n + 1) * chunk, -1:])[:, :, None]
            for part in key_words
        ]
        pairs = [pair_of(parts, dx) for dx in range(2)]
        decays = [pair_of(gates, dx) for dx in range(2)]
        both = jnp.stack([pairs[dx][0] + decays[dx][0] * pairs[dx][1] for dx in range(2)])
        decay = jnp.stack([decays[dx][0] * decays[dx][1] for dx in range(2)])
        reach = None
        for hop in range(nz - 1, 0, -1):
            send = both if reach is None else both + decay * reach
            got = along(send, -1, hop)
            reach = got if reach is None else reach + got
        found = []
        for dx in range(2):
            for_second = reach[dx]
            for_first = pairs[dx][1] + decays[dx][1] * for_second
            found += list(ordered(for_first, for_second))
        adjoints.append(found)

    half = heads_here // 2
    mine, other = y * half, (1 - y) * half

    def cut(value, start):
        return lax.dynamic_slice_in_dim(value, start, half, 0)

    first, second = ordered(cut(state_sum, mine), swap(cut(state_sum, other), 0, 1))
    first_decay, second_decay = ordered(spread_totals, swap(spread_totals, 0, 1))
    first_decay = cut(first_decay, mine)[:, :1, None]
    second_decay = cut(second_decay, mine)[:, :1, None]
    both = second_decay * first + second
    reach = None
    for hop in range(nz - 1):
        send = both if reach is None else both + second_decay * first_decay * reach
        got = along(send, 1, hop)
        reach = got if reach is None else reach + got
    keep, send = ordered(reach, first_decay * reach + first)
    state = jnp.concatenate(ordered(keep, swap(send, 0, 1)), axis=0)

    columns = pattern.shape[0] // QUAD
    own_pattern = lax.dynamic_slice_in_dim(pattern, quad * columns, columns, 0)
    share = SEL // nz
    columns = columns // CHUNKS
    results = []
    for n in range(CHUNKS):
        grads = plane(value_parts[n])
        partial_value = pl.pallas_call(
            lambda *refs, n=n: block_kernel(n * chunk, *refs),
            grid_spec=pltpu.PrefetchScalarGridSpec(
                num_scalar_prefetch=1,
                grid=(chunk,),
                in_specs=[spec(input_spikes.shape, lambda j: (0, 0))] * QUAD
                + [spec((tokens, HEAD), lambda j: (0, j))] * QUAD
                + [spec((WORDS, tokens), lambda j, n=n: (j + n * chunk, 0))] * QUAD
                + [spec((8, tokens), lambda j: (heads, 0))] * QUAD
                + [spec((1, HEAD, HEAD), lambda j: (j, 0, 0))] * QUAD,
                out_specs=spec((SEL, 2, HALF, HEAD), lambda j: (0, j, 0, 0)),
                scratch_shapes=[pltpu.VMEM((SEL * HALF, 2 * tokens), BF16)],
            ),
            out_shape=shape(SEL, columns, HALF, HEAD),
            compiler_params=params(),
            cost_estimate=cost(3 * unit // CHUNKS, 16 * mib // CHUNKS),
            name="block_kernel",
        )(own_pattern, *spikes, *grads, *key_words, *key_words, *adjoints[n])

        pieces = partial_value.reshape(nz, share, columns, HALF, HEAD)

        def piece(at):
            return lax.dynamic_index_in_dim(pieces, jnp.clip(at, 0, nz - 1), 0, keepdims=False)

        up = down = None
        for step in range(nz - 1):
            send_up = piece(nz - 1 - step + z)
            send_down = piece(step - (nz - 1 - z))
            if step:
                send_up, send_down = send_up + up, send_down + down
            up = lax.ppermute(
                send_up, "ctx", [(c, c + 2) for c in range(nctx - 2) if c // 2 <= step]
            )
            down = lax.ppermute(
                send_down, "ctx", [(c, c - 2) for c in range(2, nctx) if nz - 1 - c // 2 <= step]
            )
        summed = piece(z) + up + down

        def rows(dx, dy):
            part = lax.dynamic_slice_in_dim(summed, (y ^ dy) * (share // 2), share // 2, 0)
            return part if (dx, dy) == (0, 0) else swap(part, dx, dy)

        parts = [rows(*offset) for offset in offsets]
        parts = [jnp.where(y == 0, parts[i], parts[i ^ 1]) for i in range(QUAD)]
        parts = [jnp.where(x == 0, parts[i], parts[i ^ 2]) for i in range(QUAD)]
        results.append(jnp.stack(parts, axis=1))
    value_grad = jnp.stack(results, axis=2).reshape(share // 2, pattern.shape[0], BLK * BLK)

    h, xv = call(
        "output_kernel",
        lambda *refs: output_kernel(chunk, heads, *refs),
        [state_spec] + [flat_spec] * 4 + [cum_spec] * (1 + CHUNKS),
        [col_spec, vec_spec],
        [shape(QUAD, tokens, 8), vecs],
        cost(3 * unit, 12 * mib),
        state,
        qt,
        kt,
        values,
        grad_out,
        cum,
        *dens,
    )
    cv = vec(carried_vectors(unvec(xv), False))
    returned = [
        jnp.concatenate(
            [
                adjoints[n][i] if i == 0 else swap(adjoints[n][i], *offsets[i])
                for n in range(CHUNKS)
            ],
            axis=0,
        )
        for i in range(QUAD)
    ]
    dq, dk = pl.pallas_call(
        lambda *refs: token_kernel(chunk, heads, *refs),
        grid_spec=pltpu.PrefetchScalarGridSpec(
            num_scalar_prefetch=1,
            grid=(QUAD,),
            in_specs=[
                state_spec,
                pl.BlockSpec((1, heads, HEAD, HEAD), lambda j, turn: (j ^ turn[0], 0, 0, 0)),
                vec_spec,
            ]
            + [flat_spec] * 4
            + [cum_spec, flat_spec, col_spec]
            + [cum_spec] * CHUNKS,
            out_specs=[flat_spec, flat_spec],
        ),
        out_shape=[flat16, flat32],
        compiler_params=params(),
        cost_estimate=cost(5 * unit, 20 * mib),
        name="token_kernel",
    )(
        quad.astype(jnp.int32).reshape(1),
        state,
        jnp.stack(returned),
        z0,
        qt,
        kt,
        values,
        grad_out,
        cum,
        query_slope,
        h,
        *dens,
    )
    key_grad = call(
        "key_kernel",
        lambda *refs: key_kernel(heads, *refs),
        [flat_spec, vec_spec, cum_spec, flat_spec],
        flat_spec,
        flat16,
        cost(1, 8 * mib),
        dk,
        cv,
        cum,
        key_slope,
    )
    return (dq, key_grad, value_grad)


def solution(mesh):
    in_specs = (
        P(None, ("dp", "ctx")),
        P("tensor", ("dp", "ctx")),
        P("tensor", ("dp", "ctx")),
        P(("dp", "ctx"), "tensor"),
        P(("dp", "ctx"), "tensor"),
        P(("dp", "ctx"), "tensor"),
        P(("dp", "ctx"), "tensor"),
        P("tensor", ("dp", "ctx")),
        P("tensor", None),
    )
    out_specs = (P(("dp", "ctx"), "tensor"), P(("dp", "ctx"), "tensor"), P("ctx", "tensor", None))
    return jax.shard_map(
        per_device, mesh=mesh, in_specs=in_specs, out_specs=out_specs, check_vma=False
    )
```

```python
import jax
import jax.numpy as jnp
from jax import lax
from jax.experimental import pallas as pl
from jax.experimental.pallas import tpu as pltpu
from jax.sharding import PartitionSpec as P

HEAD = 128
WORDS = HEAD // 16
BLK = 64
HALF = BLK // 2
SEL = 16
QUAD = 4
CHUNKS = 2

F32 = jnp.float32
BF16 = jnp.bfloat16
VMEM_LIMIT = 62 * 1024 * 1024


def params():
    return pltpu.CompilerParams(vmem_limit_bytes=VMEM_LIMIT)


def cost(flops, nbytes):
    return pl.CostEstimate(flops=int(flops), bytes_accessed=int(nbytes), transcendentals=0)


def nn(a, b):
    return lax.dot_general(a, b, (((1,), (0,)), ((), ())), preferred_element_type=F32)


def nt(a, b):
    return lax.dot_general(a, b, (((1,), (1,)), ((), ())), preferred_element_type=F32)


def tn(a, b):
    return lax.dot_general(a, b, (((0,), (0,)), ((), ())), preferred_element_type=F32)


def split(a):
    high = a.astype(BF16)
    return high, (a - high.astype(F32)).astype(BF16)


def fold(a):
    return a[:, :HEAD] + a[:, HEAD:]


def unpack(words):
    tokens = words.shape[1]
    spread = jnp.broadcast_to(words[:, None, :], (WORDS, 16, tokens))
    shifts = lax.broadcasted_iota(jnp.int32, (WORDS, 16, tokens), 1)
    bits = jnp.bitwise_and(jnp.right_shift(spread, shifts), 1)
    return bits.reshape(HEAD, tokens).astype(F32)


def causal(shape, token_axis):
    return lax.broadcasted_iota(jnp.int32, shape, token_axis) >= lax.broadcasted_iota(
        jnp.int32, shape, 1 - token_axis
    )


def lanes(i):
    return slice(i * HEAD, (i + 1) * HEAD)


def rows_of(vector):
    high, low = split(vector)
    low2 = (vector - high.astype(F32) - low.astype(F32)).astype(BF16)
    n = vector.shape[1]
    return jnp.concatenate([high, low, low2, jnp.zeros((13, n), BF16)], axis=0)


def key_sums_kernel(heads, kw, cum, out):
    for i in range(heads):
        row = cum[0, i : i + 1, :]
        tail = jnp.exp(row[:, -1:] - row)
        k = unpack(kw[i * WORDS : (i + 1) * WORDS, :]).astype(BF16)
        out[0, i : i + 1, :] = jnp.sum(nt(rows_of(tail), k), axis=0, keepdims=True)


def state_kernel(heads, kw, v, cum, y_out, kt_out):
    for i in range(heads):
        row = cum[0, i : i + 1, :]
        k = unpack(kw[i * WORDS : (i + 1) * WORDS, :])
        kt_out[:, lanes(i)] = jnp.transpose(k).astype(BF16)
        high, low = split(k * jnp.exp(row[:, -1:] - row))
        value = v[:, lanes(i)]
        y_out[i] = nn(high, value) + nn(low, value)


def weight_kernel(heads, qw, kt, cum, wt_out, den_out, qt_out):
    tokens = kt.shape[0]
    cols = jnp.transpose(cum[0])
    after = causal((tokens, tokens), 1)
    for i in range(heads):
        row = cum[0, i : i + 1, :]
        col = cols[:, i : i + 1]
        q = unpack(qw[i * WORDS : (i + 1) * WORDS, :])
        qt_out[:, lanes(i)] = jnp.transpose(q).astype(BF16)
        decay = jnp.where(after, jnp.exp(jnp.minimum(row - col, 0.0)), 0.0)
        w = nn(kt[:, lanes(i)], q.astype(BF16)) * decay
        wt_out[i] = w.astype(BF16)
        den_out[0, i : i + 1, :] = jnp.sum(w, axis=0, keepdims=True)


def start_kernel(z, received, up, order, down_out, send_out):
    second = received[1, :, :HEAD, :]
    down = received[0, :, :HEAD, :] + received[0, :, HEAD : HEAD + 1, :] * second
    down_out[0] = down
    send_out[0] = jnp.where(z[0] == 0, up[0], down)


def local_kernel(heads, wt, v, out):
    for i in range(heads):
        out[:, lanes(i)] = tn(wt[i], v[:, lanes(i)])


def adjoint_kernel(start, heads, qw, do, cum, den_local, z0, wt, *refs):
    den_out, x_out, dv_out = refs[-3:]
    tokens = do.shape[0]
    rows = []
    qs = []
    for i in range(heads):
        at = start + i
        row = cum[0, at : at + 1, :]
        q = unpack(qw[i * WORDS : (i + 1) * WORDS, :]).astype(BF16)
        qs.append(q)
        carried = jnp.sum(nn(rows_of(z0[0, at : at + 1, :]), q), axis=0, keepdims=True)
        rows.append(1.0 + den_local[0, at : at + 1, :] + jnp.exp(row) * carried)
    rows = rows + [jnp.ones((1, tokens), F32)] * (8 - heads)
    den = jnp.concatenate(rows, axis=0)
    den_out[0] = den
    inverse = jnp.transpose(1.0 / den)
    leads = jnp.exp(jnp.transpose(cum[0]))
    for i in range(heads):
        g = do[:, lanes(i)].astype(F32) * inverse[:, i : i + 1]
        lead = leads[:, start + i : start + i + 1]
        x_out[0, i, :HEAD, :] = fold(nn(qs[i], jnp.concatenate(split(g * lead), axis=1)))
        x_out[0, i, HEAD:, :] = jnp.broadcast_to(lead[-1:, :], (8, HEAD))
        dv_out[0, 0, :, lanes(i)] = nn(wt[i], g.astype(BF16))


def output_kernel(chunk, heads, y, keep, got, local, qt, do, cum, *refs):
    dens, (h_out, xv_out) = refs[:-3], refs[-2:]
    cols = jnp.transpose(cum[0])
    inverses = [jnp.transpose(1.0 / den[0]) for den in dens]
    kept = pl.program_id(0) // 2 == y[0]
    for i in range(heads):
        col = cols[:, i : i + 1]
        inverse = inverses[i // chunk][:, i % chunk : i % chunk + 1]
        lead = jnp.exp(col)
        q = qt[:, lanes(i)]
        grad = do[:, lanes(i)].astype(F32)
        state = jnp.where(kept, keep[i], got[i])
        carried = fold(nn(q, jnp.concatenate(split(state), axis=1)))
        o = (local[:, lanes(i)] + lead * carried) * inverse
        h = -jnp.sum(grad * o, axis=1, keepdims=True) * inverse
        h_out[0, :, i : i + 1] = h
        xv_out[0, i : i + 1, :] = jnp.sum(q.astype(F32) * (lead * h), axis=0, keepdims=True)


def token_kernel(chunk, heads, y, quad, keep, got, z0, qt, kt, v, do, cum, slope, h_in, *refs):
    dens, adjoints, (dq_out, dk_out) = refs[:CHUNKS], refs[CHUNKS:-2], refs[-2:]
    offset = pl.program_id(0) ^ quad[0]
    tokens = v.shape[0]
    cols = jnp.transpose(cum[0])
    inverses = [jnp.transpose(1.0 / den[0]) for den in dens]
    before = causal((tokens, tokens), 0)
    kept = pl.program_id(0) // 2 == y[0]
    for i in range(heads):
        row = cum[0, i : i + 1, :]
        col = cols[:, i : i + 1]
        inverse = inverses[i // chunk][:, i % chunk : i % chunk + 1]
        lead = jnp.exp(col)
        tail = jnp.exp(col[-1:, :] - col)
        value = v[:, lanes(i)]
        decay = jnp.where(before, jnp.exp(jnp.minimum(col - row, 0.0)), 0.0)
        h = h_in[0, :, i : i + 1]
        g = (do[:, lanes(i)].astype(F32) * inverse).astype(BF16)
        r = ((nt(g, value) + h) * decay).astype(BF16)
        state = jnp.where(kept, keep[i], got[i])
        back = fold(nt(g, jnp.concatenate(split(state), axis=0))) + h * z0[0, i : i + 1, :]
        dq = nn(r, kt[:, lanes(i)]) + lead * back
        dq_out[:, lanes(i)] = (slope[:, lanes(i)].astype(F32) * dq).astype(BF16)
        adjoint = adjoints[QUAD * (i // chunk)][i % chunk]
        for at in range(1, QUAD):
            adjoint = jnp.where(offset == at, adjoints[QUAD * (i // chunk) + at][i % chunk], adjoint)
        carried = fold(nt(value, jnp.concatenate(split(adjoint), axis=0)))
        dk_out[:, lanes(i)] = tn(r, qt[:, lanes(i)]) + tail * carried


def key_kernel(heads, dk, cv, cum, slope, out):
    cols = jnp.transpose(cum[0])
    for i in range(heads):
        col = cols[:, i : i + 1]
        tail = jnp.exp(col[-1:, :] - col)
        total = dk[:, lanes(i)] + tail * cv[0, i : i + 1, :]
        out[:, lanes(i)] = (slope[:, lanes(i)].astype(F32) * total).astype(BF16)


def block_kernel(start, quad, core, pattern, *refs):
    keep_out, send_out, *adjoint_outs = refs[-6 - QUAD : -4]
    flags, lines, others, found = refs[-4:]
    pieces, (grads, parts, reach), other_pieces = refs[:QUAD], refs[QUAD : QUAD + 3], refs[QUAD + 3 : -7 - QUAD]
    tokens = grads.shape[2]
    key_rows = others.shape[1] - 8
    ncore = 1 + len(other_pieces)
    spike_rows = lines.shape[1] // ncore
    step = pl.program_id(0)
    shifts = 2 * lax.broadcasted_iota(jnp.int32, (8, tokens), 0)
    low = lax.broadcasted_iota(jnp.int32, (tokens, HEAD), 1) < BLK

    @pl.when(step == 0)
    def _():
        for i in range(QUAD):
            source = quad[0] ^ i
            others[source] = pieces[i][spike_rows:, :]
            for k in range(ncore):
                part = other_pieces[k - 1][i] if k else pieces[i][:spike_rows, :]
                rows = pl.multiple_of(lax.rem(core[0] + ncore - k, ncore) * spike_rows, spike_rows)
                lines[source, pl.ds(rows, spike_rows), :] = part.astype(jnp.int32)

    values = []
    for source in range(QUAD):
        if source % 2:
            adjoint = reach[source // 2, 0]
        else:
            adjoint = parts[source + 1, 0, :HEAD, :] + parts[source + 1, 0, HEAD : HEAD + 1, :] * reach[source // 2, 0]
        found[source] = adjoint
        row = others[source, pl.ds(key_rows + start + step, 1), :]
        words = others[source, pl.ds(pl.multiple_of((start + step) * WORDS, WORDS), WORDS), :]
        k = unpack(words.astype(jnp.int32)) * jnp.exp(row[:, -1:] - row)
        carried = fold(tn(k.astype(BF16), jnp.concatenate(split(adjoint), axis=1)))
        values.append((grads[source, 0] + carried).astype(BF16).astype(F32))
    for i in range(QUAD):
        adjoint_outs[i][0] = found[quad[0] ^ i]
    for side in range(2):
        total = None
        for source in range(QUAD):
            grad = values[source]
            turned = jnp.concatenate([grad[:, BLK:], grad[:, :BLK]], axis=1)
            even, odd = (grad, turned) if side == 0 else (turned, grad)
            right = jnp.concatenate(
                [jnp.where(low, even, 0.0).astype(BF16), jnp.where(low, 0.0, odd).astype(BF16)], axis=0
            )
            for s in range(SEL):
                first = pattern[2 * (start + step) + side, s] * (BLK // 16)
                for parity in range(2):
                    flag_parts = []
                    for word in range(BLK // 16):
                        line = lines[source, pl.ds(first + word, 1), :]
                        spread = jnp.broadcast_to(line, (8, tokens))
                        flag_parts.append(jnp.bitwise_and(jnp.right_shift(spread, shifts + parity), 1))
                    bits = jnp.concatenate(flag_parts, axis=0).astype(F32).astype(BF16)
                    flags[s * HALF : (s + 1) * HALF, parity * tokens : (parity + 1) * tokens] = bits
            part = nn(flags[...], right)
            total = part if total is None else total + part
        total = total.reshape(SEL, HALF, HEAD)
        keep_out[:, side] = total[: SEL // 2]
        send_out[:, side] = total[SEL // 2 :]


def finish_kernel(quad, *refs):
    parts, out = refs[:-1], refs[-1]
    rows = parts[0].shape[1]

    def place(source, offset):
        @pl.when(quad[0] ^ offset == source)
        def _():
            for n in range(CHUNKS):
                first = (source * CHUNKS + n) * rows
                for i in range(HALF):
                    out[0, first : first + rows, lanes(i)] = parts[n * QUAD + offset][0, :, i, :]

    for source in range(QUAD):
        for offset in range(QUAD):
            place(source, offset)


def per_device(
    input_spikes,
    query_spikes,
    key_spikes,
    values,
    query_slope,
    key_slope,
    grad_out,
    log_gate,
    pattern,
):
    tokens, width = values.shape
    heads_here = width // HEAD
    heads = heads_here // QUAD
    chunk = heads // CHUNKS
    nctx, ndp = lax.axis_size("ctx"), lax.axis_size("dp")
    nz = nctx // 2
    x, place = lax.axis_index("dp"), lax.axis_index("ctx")
    y, z = place % 2, place // 2
    quad = (2 * x + y).astype(jnp.int32).reshape(1)
    planes = [[d * nctx + 2 * c + i for d in range(ndp) for i in range(2)] for c in range(nz)]

    gate_sums = jnp.cumsum(log_gate, axis=1)
    totals = jnp.exp(gate_sums[:, -1])
    cum = gate_sums.reshape(QUAD, heads, tokens)
    cum = jnp.pad(cum, ((0, 0), (0, 8 - heads), (0, 0)))

    def spec(block, index):
        return pl.BlockSpec(block, lambda j, *refs: index(j))

    word_spec = spec((heads * WORDS, tokens), lambda j: (j, 0))
    flat_spec = spec((tokens, heads * HEAD), lambda j: (0, j))
    cum_spec = spec((1, 8, tokens), lambda j: (j, 0, 0))
    vec_spec = spec((1, 8, HEAD), lambda j: (j, 0, 0))
    state_spec = spec((heads, HEAD, HEAD), lambda j: (j, 0, 0))
    wt_spec = spec((heads, tokens, tokens), lambda j: (j, 0, 0))
    col_spec = spec((1, tokens, 8), lambda j: (j, 0, 0))

    def shape(*dims, kind=F32):
        return jax.ShapeDtypeStruct(dims, kind)

    flat16 = shape(tokens, width, kind=BF16)
    flat32 = shape(tokens, width)
    states = shape(heads_here, HEAD, HEAD)
    vecs = shape(QUAD, 8, HEAD)
    cums = shape(QUAD, 8, tokens)
    unit = 2 * tokens * tokens * HEAD * heads_here
    mib = 1 << 20

    def call(name, kernel, in_specs, out_specs, out_shape, estimate, *args, scalars=0, aliases={}):
        def body(*refs):
            kernel(*refs)

        body.__name__ = name
        return pl.pallas_call(
            body,
            grid_spec=pltpu.PrefetchScalarGridSpec(
                num_scalar_prefetch=scalars, grid=(QUAD,), in_specs=in_specs, out_specs=out_specs
            ),
            out_shape=out_shape,
            input_output_aliases=aliases,
            compiler_params=params(),
            cost_estimate=estimate,
            name=name,
        )(*args)

    def swap(value):
        return lax.ppermute(value, "ctx", [(c, c ^ 1) for c in range(nctx)])

    def across(value, offset):
        pairs = [
            (d * nctx + c, (d ^ (offset // 2)) * nctx + (c ^ (offset % 2)))
            for d in range(ndp)
            for c in range(nctx)
        ]
        return lax.ppermute(value, ("dp", "ctx"), pairs)

    def plane(value):
        return lax.all_to_all(value, ("dp", "ctx"), 0, 0, axis_index_groups=planes, tiled=True)

    def vec(a):
        return jnp.pad(a.reshape(QUAD, heads, HEAD), ((0, 0), (0, 8 - heads), (0, 0)))

    def unvec(a):
        return a[:, :heads].reshape(heads_here, HEAD)

    def ordered(own, got):
        return jnp.where(y == 0, own, got), jnp.where(y == 0, got, own)

    def carried_vectors(vector, forward):
        message = jnp.concatenate([vector, jnp.broadcast_to(totals[:, None], vector.shape)], axis=0)
        message = jnp.broadcast_to(message[None], (nctx,) + message.shape)
        parts = lax.all_to_all(message, "ctx", 0, 0, tiled=True)
        reach = jnp.zeros_like(vector)
        for at in range(nctx) if forward else range(nctx - 1, -1, -1):
            inside = at < place if forward else at > place
            reach = jnp.where(inside, parts[at, heads_here:] * reach + parts[at, :heads_here], reach)
        return reach, parts[:, heads_here:, 0]

    key_sum = call(
        "key_sums_kernel",
        lambda *refs: key_sums_kernel(heads, *refs),
        [word_spec, cum_spec],
        vec_spec,
        vecs,
        cost(1, 1),
        key_spikes,
        cum,
    )
    z0, decays = carried_vectors(unvec(key_sum), True)
    z0 = vec(z0)
    first_total = lax.dynamic_index_in_dim(decays, 2 * z, 0, keepdims=False)
    second_total = lax.dynamic_index_in_dim(decays, 2 * z + 1, 0, keepdims=False)

    ncore, core = lax.axis_size("tensor"), lax.axis_index("tensor")
    spike_rows = input_spikes.shape[0] // ncore
    spike_words = lax.dynamic_slice_in_dim(input_spikes, core * spike_rows, spike_rows, 0).astype(F32)
    spike_words = jnp.broadcast_to(spike_words[None], (QUAD,) + spike_words.shape)
    key_words = key_spikes.reshape(QUAD, heads * WORDS, tokens).astype(F32)
    key_words = jnp.concatenate([spike_words, key_words, cum], axis=1)
    pieces = []
    for i in range(QUAD):
        part = lax.dynamic_index_in_dim(key_words, quad[0] ^ i, 0, keepdims=False)
        pieces.append(across(part, i) if i else part)
    other_pieces = jnp.stack([piece[:spike_rows] for piece in pieces])
    other_pieces = [
        lax.ppermute(other_pieces, "tensor", [(c, (c + k) % ncore) for c in range(ncore)])
        for k in range(1, ncore)
    ]

    state_sum, kt = call(
        "state_kernel",
        lambda *refs: state_kernel(heads, *refs),
        [word_spec, flat_spec, cum_spec],
        [state_spec, flat_spec],
        [states, flat16],
        cost(1, 1),
        key_spikes,
        values,
        cum,
    )
    wt, den_local, qt = call(
        "weight_kernel",
        lambda *refs: weight_kernel(heads, *refs),
        [word_spec, flat_spec, cum_spec],
        [wt_spec, cum_spec, flat_spec],
        [shape(heads_here, tokens, tokens, kind=BF16), cums, flat16],
        cost(1, 1),
        query_spikes,
        kt,
        cum,
    )
    dens, adjoint_sums, value_parts = [], [], None
    anywhere = pl.BlockSpec(memory_space=pl.ANY)
    for n in range(CHUNKS):
        extra = pieces if n == 0 else [value_parts]
        den, adjoint_sum, value_parts = call(
            "adjoint_kernel",
            lambda *refs, n=n: adjoint_kernel(n * chunk, chunk, *refs),
            [
                spec((chunk * WORDS, tokens), lambda j, n=n: (j * CHUNKS + n, 0)),
                spec((tokens, chunk * HEAD), lambda j, n=n: (0, j * CHUNKS + n)),
                cum_spec,
                cum_spec,
                vec_spec,
                spec((chunk, tokens, tokens), lambda j, n=n: (j * CHUNKS + n, 0, 0)),
            ]
            + [anywhere] * len(extra),
            [
                cum_spec,
                spec((1, chunk, HEAD + 8, HEAD), lambda j: (j, 0, 0, 0)),
                spec((1, 1, tokens, chunk * HEAD), lambda j, n=n: (j, n, 0, 0)),
            ],
            [cums, shape(QUAD, chunk, HEAD + 8, HEAD), shape(QUAD, CHUNKS, tokens, chunk * HEAD)],
            cost(1, 1),
            query_spikes,
            grad_out,
            cum,
            den_local,
            z0,
            wt,
            *extra,
            aliases={6: 2} if n else {},
        )
        dens.append(den)
        adjoint_sums.append(adjoint_sum)

    local = call(
        "local_kernel",
        lambda wt, v, *refs: local_kernel(heads, wt, v, refs[-1]),
        [wt_spec, flat_spec] + [anywhere] * len([adjoint_sums[-1], *other_pieces]),
        flat_spec,
        flat32,
        cost(1, 1),
        wt,
        values,
        adjoint_sums[-1],
        *other_pieces,
    )

    half = heads_here // 2
    mine, other = y * half, (1 - y) * half

    def cut(value, start):
        return lax.dynamic_slice_in_dim(value, start, half, 0)

    first, second = ordered(cut(state_sum, mine), swap(cut(state_sum, other)))
    first_decay = cut(first_total, mine)[:, None, None]
    second_decay = cut(second_total, mine)[:, None, None]
    state_both = second_decay * first + second
    state_decay = second_decay * first_decay
    part_size = half // CHUNKS

    reaches, adjoint_parts = [], []
    for n in range(CHUNKS):
        received = plane(adjoint_sums[n])
        parts = received.reshape(2, 2, chunk, HEAD + 8, HEAD)
        gates = parts[:, :, :, HEAD : HEAD + 1, :1]
        down_decay = gates[:, 0] * gates[:, 1]
        size = (2, chunk, HEAD, HEAD)
        up = state_both[n * part_size : (n + 1) * part_size].reshape(size)
        size_spec = spec((1,) + size[1:], lambda j: (j, 0, 0, 0))
        down, send = pl.pallas_call(
            start_kernel,
            grid_spec=pltpu.PrefetchScalarGridSpec(
                num_scalar_prefetch=1,
                grid=(2,),
                in_specs=[
                    spec((2, chunk, HEAD + 8, HEAD), lambda j: (j, 0, 0, 0)),
                    size_spec,
                    anywhere,
                ],
                out_specs=[size_spec, size_spec],
            ),
            out_shape=[shape(*size), shape(*size)],
            compiler_params=params(),
            cost_estimate=cost(1, 1),
            name="start_kernel",
        )(z.astype(jnp.int32).reshape(1), received, up, local)
        up_decay = state_decay[n * part_size : (n + 1) * part_size].reshape(down_decay.shape)
        reach = None
        for hop in range(nz - 1):
            if reach is not None:
                send = jnp.where(z == hop, up, down) + jnp.where(z == hop, up_decay, down_decay) * reach
            pairs = []
            for c in range(nctx):
                if c // 2 == hop:
                    pairs.append((c, c + 2))
                elif c // 2 == nz - 1 - hop:
                    pairs.append((c, c - 2))
            got = lax.ppermute(send, "ctx", pairs)
            if reach is None:
                reach = got
                reach_up = jnp.where(z == hop + 1, got, 0.0)
                reach_down = jnp.where(z == nz - 2 - hop, got, 0.0)
            else:
                reach = got
                reach_up = jnp.where(z == hop + 1, got, reach_up)
                reach_down = jnp.where(z == nz - 2 - hop, got, reach_down)
        reaches.append(reach_up.reshape(part_size, HEAD, HEAD))
        adjoint_parts.append((received, reach_down))
    reach = jnp.concatenate(reaches, axis=0)
    keep, send = ordered(reach, first_decay * reach + first)
    state = [y.astype(jnp.int32).reshape(1), keep, swap(send)]

    columns = pattern.shape[0] // QUAD
    share = SEL // nz
    own_pattern = lax.dynamic_slice_in_dim(pattern, quad[0] * columns, columns, 0)
    order = jnp.arange(nz, dtype=jnp.int32)
    turned = sum((order // (nz >> (bit + 1))) % 2 << bit for bit in range(nz.bit_length() - 1))
    order = ((z ^ turned)[:, None] * share + jnp.arange(share, dtype=jnp.int32)[None, :]).reshape(SEL)
    own_pattern = jnp.take(own_pattern, order, axis=1)
    columns = columns // CHUNKS
    value_parts = plane(value_parts)
    results, adjoints = [], []
    for n in range(CHUNKS):
        half_spec = spec((SEL // 2, 2, HALF, HEAD), lambda j: (0, j, 0, 0))
        half_shape = shape(SEL // 2, columns, HALF, HEAD)
        after = adjoints[-1][0] if adjoints else adjoint_parts[n][1]
        summed, send, *adjoint = pl.pallas_call(
            lambda *refs, n=n: block_kernel(n * chunk, *refs),
            grid_spec=pltpu.PrefetchScalarGridSpec(
                num_scalar_prefetch=3,
                grid=(chunk,),
                in_specs=[spec(piece.shape, lambda j: (0, 0)) for piece in pieces]
                + [
                    spec((QUAD, 1, tokens, HEAD), lambda j, n=n: (0, n, 0, j)),
                    spec((QUAD, 1, HEAD + 8, HEAD), lambda j: (0, j, 0, 0)),
                    spec((2, 1, HEAD, HEAD), lambda j: (0, j, 0, 0)),
                ]
                + [spec(piece.shape, lambda j: (0, 0, 0)) for piece in other_pieces]
                + [anywhere],
                out_specs=[half_spec, half_spec] + [spec((1, HEAD, HEAD), lambda j: (j, 0, 0))] * QUAD,
                scratch_shapes=[
                    pltpu.VMEM((SEL * HALF, 2 * tokens), BF16),
                    pltpu.VMEM((QUAD, input_spikes.shape[0], tokens), jnp.int32),
                    pltpu.VMEM((QUAD, pieces[0].shape[0] - spike_rows, tokens), F32),
                    pltpu.VMEM((QUAD, HEAD, HEAD), F32),
                ],
            ),
            out_shape=[half_shape, half_shape] + [shape(chunk, HEAD, HEAD)] * QUAD,
            compiler_params=params(),
            cost_estimate=cost(1, 40 * mib),
            name="block_kernel",
        )(
            quad,
            core.astype(jnp.int32).reshape(1),
            own_pattern,
            *pieces,
            value_parts,
            *adjoint_parts[n],
            *other_pieces,
            after,
        )
        adjoints.append(adjoint)

        bit = 1
        while True:
            summed = summed + lax.ppermute(send, "ctx", [(c, c ^ (2 * bit)) for c in range(nctx)])
            bit *= 2
            if bit == nz:
                break
            rest = summed.shape[0] // 2
            summed, send = summed[:rest], summed[rest:]
        for i in range(QUAD):
            part = lax.dynamic_slice_in_dim(summed, (y ^ (i % 2)) * (share // 2), share // 2, 0)
            results.append(across(part, i) if i else part)
    part_spec = spec((1, columns, HALF, HEAD), lambda j: (j, 0, 0, 0))
    value_grad = pl.pallas_call(
        finish_kernel,
        grid_spec=pltpu.PrefetchScalarGridSpec(
            num_scalar_prefetch=1,
            grid=(share // 2,),
            in_specs=[part_spec] * (CHUNKS * QUAD),
            out_specs=spec((1, pattern.shape[0], BLK * BLK), lambda j: (j, 0, 0)),
        ),
        out_shape=shape(share // 2, pattern.shape[0], BLK * BLK),
        compiler_params=params(),
        cost_estimate=cost(1, 4 * mib),
        name="finish_kernel",
    )(quad, *results)

    part_spec = spec((heads, HEAD, HEAD), lambda j: (j % 2, 0, 0))
    h, xv = call(
        "output_kernel",
        lambda *refs: output_kernel(chunk, heads, *refs),
        [part_spec] * 2 + [flat_spec] * 3 + [cum_spec] * (1 + CHUNKS) + [anywhere],
        [col_spec, vec_spec],
        [shape(QUAD, tokens, 8), vecs],
        cost(1, 40 * mib),
        *state,
        local,
        qt,
        grad_out,
        cum,
        *dens,
        adjoints[-1][0],
        scalars=1,
    )
    cv = vec(carried_vectors(unvec(xv), False)[0])
    returned = [across(adjoint[i], i) if i else adjoint[i] for adjoint in adjoints for i in range(QUAD)]
    dq, dk = call(
        "token_kernel",
        lambda *refs: token_kernel(chunk, heads, *refs),
        [part_spec, part_spec, vec_spec]
        + [flat_spec] * 4
        + [cum_spec, flat_spec, col_spec]
        + [cum_spec] * CHUNKS
        + [spec((chunk, HEAD, HEAD), lambda j: (0, 0, 0))] * (CHUNKS * QUAD),
        [flat_spec, flat_spec],
        [flat16, flat32],
        cost(1, 60 * mib),
        state[0],
        quad,
        *state[1:],
        z0,
        qt,
        kt,
        values,
        grad_out,
        cum,
        query_slope,
        h,
        *dens,
        *returned,
        scalars=2,
    )
    key_grad = call(
        "key_kernel",
        lambda *refs: key_kernel(heads, *refs),
        [flat_spec, vec_spec, cum_spec, flat_spec],
        flat_spec,
        flat16,
        cost(1, 8 * mib),
        dk,
        cv,
        cum,
        key_slope,
    )
    return (dq, key_grad, value_grad)


def solution(mesh):
    in_specs = (
        P(None, ("dp", "ctx")),
        P("tensor", ("dp", "ctx")),
        P("tensor", ("dp", "ctx")),
        P(("dp", "ctx"), "tensor"),
        P(("dp", "ctx"), "tensor"),
        P(("dp", "ctx"), "tensor"),
        P(("dp", "ctx"), "tensor"),
        P("tensor", ("dp", "ctx")),
        P("tensor", None),
    )
    out_specs = (P(("dp", "ctx"), "tensor"), P(("dp", "ctx"), "tensor"), P("ctx", "tensor", None))
    return jax.shard_map(
        per_device, mesh=mesh, in_specs=in_specs, out_specs=out_specs, check_vma=False
    )
```

```python
import jax
import jax.numpy as jnp
from jax import lax
from jax.experimental import pallas as pl
from jax.experimental.pallas import tpu as pltpu
from jax.sharding import PartitionSpec as P

HEAD = 128
WORDS = HEAD // 16
BLK = 64
HALF = BLK // 2
SEL = 16
QUAD = 4
CHUNKS = 2

F32 = jnp.float32
BF16 = jnp.bfloat16
VMEM_LIMIT = 62 * 1024 * 1024


def params():
    return pltpu.CompilerParams(vmem_limit_bytes=VMEM_LIMIT)


def cost(flops, nbytes):
    return pl.CostEstimate(flops=int(flops), bytes_accessed=int(nbytes), transcendentals=0)


def nn(a, b):
    return lax.dot_general(a, b, (((1,), (0,)), ((), ())), preferred_element_type=F32)


def nt(a, b):
    return lax.dot_general(a, b, (((1,), (1,)), ((), ())), preferred_element_type=F32)


def tn(a, b):
    return lax.dot_general(a, b, (((0,), (0,)), ((), ())), preferred_element_type=F32)


def split(a):
    high = a.astype(BF16)
    return high, (a - high.astype(F32)).astype(BF16)


def fold(a):
    return a[:, :HEAD] + a[:, HEAD:]


def unpack(words):
    tokens = words.shape[1]
    spread = jnp.broadcast_to(words[:, None, :], (WORDS, 16, tokens))
    shifts = lax.broadcasted_iota(jnp.int32, (WORDS, 16, tokens), 1)
    bits = jnp.bitwise_and(jnp.right_shift(spread, shifts), 1)
    return bits.reshape(HEAD, tokens).astype(F32)


def causal(shape, token_axis):
    return lax.broadcasted_iota(jnp.int32, shape, token_axis) >= lax.broadcasted_iota(
        jnp.int32, shape, 1 - token_axis
    )


def lanes(i):
    return slice(i * HEAD, (i + 1) * HEAD)


def rows_of(vector):
    high, low = split(vector)
    low2 = (vector - high.astype(F32) - low.astype(F32)).astype(BF16)
    n = vector.shape[1]
    return jnp.concatenate([high, low, low2, jnp.zeros((13, n), BF16)], axis=0)


def put_message(out, i, vector, total):
    copies = out.shape[0]
    out[:, 0, i : i + 1, :] = jnp.broadcast_to(vector[None], (copies, 1, HEAD))
    out[:, 0, 8 + i : 9 + i, :] = jnp.broadcast_to(total[None], (copies, 1, HEAD))


def key_sums_kernel(heads, kw, cum, out):
    for i in range(heads):
        row = cum[0, i : i + 1, :]
        tail = jnp.exp(row[:, -1:] - row)
        k = unpack(kw[i * WORDS : (i + 1) * WORDS, :]).astype(BF16)
        vector = jnp.sum(nt(rows_of(tail), k), axis=0, keepdims=True)
        put_message(out, i, vector, jnp.exp(row[:, -1:]))


def state_kernel(heads, kw, v, cum, y_out):
    for i in range(heads):
        row = cum[0, i : i + 1, :]
        k = unpack(kw[i * WORDS : (i + 1) * WORDS, :])
        high, low = split(k * jnp.exp(row[:, -1:] - row))
        value = v[:, lanes(i)]
        y_out[i] = nn(high, value) + nn(low, value)


def weight_kernel(heads, qw, kw, cum, wt_out, den_out, qt_out, kt_out):
    tokens = kt_out.shape[0]
    cols = jnp.transpose(cum[0])
    after = causal((tokens, tokens), 1)
    for i in range(heads):
        row = cum[0, i : i + 1, :]
        col = cols[:, i : i + 1]
        q = unpack(qw[i * WORDS : (i + 1) * WORDS, :])
        kt = jnp.transpose(unpack(kw[i * WORDS : (i + 1) * WORDS, :])).astype(BF16)
        kt_out[:, lanes(i)] = kt
        qt_out[:, lanes(i)] = jnp.transpose(q).astype(BF16)
        decay = jnp.where(after, jnp.exp(jnp.minimum(row - col, 0.0)), 0.0)
        w = nn(kt, q.astype(BF16)) * decay
        wt_out[i] = w.astype(BF16)
        den_out[0, i : i + 1, :] = jnp.sum(w, axis=0, keepdims=True)


def start_kernel(z, received, up, order, down_out, send_out):
    second = received[1, :, :HEAD, :]
    down = received[0, :, :HEAD, :] + received[0, :, HEAD : HEAD + 1, :] * second
    down_out[0] = down
    send_out[0] = jnp.where(z[0] == 0, up[0], down)


def turn_kernel(sizes, z, y, first, decay, order, *refs):
    hops, (keep_out, send_out) = refs[:-2], refs[-2:]
    count = len(hops) // CHUNKS
    for n in range(CHUNKS):
        for i in range(sizes[n]):
            at = n * sizes[0] + i
            reach = jnp.zeros((HEAD, HEAD), F32)
            for hop in range(count):
                reach = jnp.where(z[0] == hop + 1, hops[n * count + hop][i], reach)
            later = decay[at] * reach + first[at]
            keep_out[at] = jnp.where(y[0] == 0, reach, later)
            send_out[at] = jnp.where(y[0] == 0, later, reach)


def sum_kernel(y, *refs):
    terms, (own_out, other_out) = refs[:-3], refs[-2:]
    own_out[...] = sum((term[...] for term in terms[2::2]), terms[0][...])
    other_out[...] = sum((term[...] for term in terms[3::2]), terms[1][...])


def local_kernel(heads, wt, v, out):
    for i in range(heads):
        out[:, lanes(i)] = tn(wt[i], v[:, lanes(i)])


def adjoint_kernel(start, heads, qw, do, cum, den_local, z0, wt, den_out, x_out, dv_out):
    tokens = do.shape[0]
    rows = []
    qs = []
    for i in range(heads):
        at = start + i
        row = cum[0, at : at + 1, :]
        q = unpack(qw[i * WORDS : (i + 1) * WORDS, :]).astype(BF16)
        qs.append(q)
        carried = jnp.sum(nn(rows_of(z0[0, at : at + 1, :]), q), axis=0, keepdims=True)
        rows.append(1.0 + den_local[0, at : at + 1, :] + jnp.exp(row) * carried)
    rows = rows + [jnp.ones((1, tokens), F32)] * (8 - heads)
    den = jnp.concatenate(rows, axis=0)
    den_out[0] = den
    inverse = jnp.transpose(1.0 / den)
    leads = jnp.exp(jnp.transpose(cum[0]))
    for i in range(heads):
        g = do[:, lanes(i)].astype(F32) * inverse[:, i : i + 1]
        lead = leads[:, start + i : start + i + 1]
        x_out[0, i, :HEAD, :] = fold(nn(qs[i], jnp.concatenate(split(g * lead), axis=1)))
        x_out[0, i, HEAD:, :] = jnp.broadcast_to(lead[-1:, :], (8, HEAD))
        dv_out[0, :, lanes(i)] = nn(wt[i], g.astype(BF16))


def output_kernel(chunk, heads, y, keep, got, local, qt, do, cum, *refs):
    dens, (h_out, xv_out) = refs[:CHUNKS], refs[-2:]
    cols = jnp.transpose(cum[0])
    inverses = [jnp.transpose(1.0 / den[0]) for den in dens]
    kept = pl.program_id(0) // 2 == y[0]
    for i in range(heads):
        col = cols[:, i : i + 1]
        inverse = inverses[i // chunk][:, i % chunk : i % chunk + 1]
        lead = jnp.exp(col)
        q = qt[:, lanes(i)]
        grad = do[:, lanes(i)].astype(F32)
        state = jnp.where(kept, keep[i], got[i])
        carried = fold(nn(q, jnp.concatenate(split(state), axis=1)))
        o = (local[:, lanes(i)] + lead * carried) * inverse
        h = -jnp.sum(grad * o, axis=1, keepdims=True) * inverse
        h_out[0, :, i : i + 1] = h
        vector = jnp.sum(q.astype(F32) * (lead * h), axis=0, keepdims=True)
        put_message(xv_out, i, vector, lead[-1:, :])


def token_kernel(chunk, heads, y, keep, got, z0, qt, kt, v, do, cum, slope, h_in, *refs):
    dens, adjoints, (dq_out, dk_out) = refs[:CHUNKS], refs[CHUNKS:-2], refs[-2:]
    tokens = v.shape[0]
    cols = jnp.transpose(cum[0])
    inverses = [jnp.transpose(1.0 / den[0]) for den in dens]
    before = causal((tokens, tokens), 0)
    kept = pl.program_id(0) // 2 == y[0]
    for i in range(heads):
        row = cum[0, i : i + 1, :]
        col = cols[:, i : i + 1]
        inverse = inverses[i // chunk][:, i % chunk : i % chunk + 1]
        lead = jnp.exp(col)
        tail = jnp.exp(col[-1:, :] - col)
        value = v[:, lanes(i)]
        decay = jnp.where(before, jnp.exp(jnp.minimum(col - row, 0.0)), 0.0)
        h = h_in[0, :, i : i + 1]
        g = (do[:, lanes(i)].astype(F32) * inverse).astype(BF16)
        r = ((nt(g, value) + h) * decay).astype(BF16)
        state = jnp.where(kept, keep[i], got[i])
        back = fold(nt(g, jnp.concatenate(split(state), axis=0))) + h * z0[0, i : i + 1, :]
        dq = nn(r, kt[:, lanes(i)]) + lead * back
        dq_out[:, lanes(i)] = (slope[:, lanes(i)].astype(F32) * dq).astype(BF16)
        adjoint = adjoints[i // chunk][0, i % chunk]
        carried = fold(nt(value, jnp.concatenate(split(adjoint), axis=0)))
        dk_out[:, lanes(i)] = tn(r, qt[:, lanes(i)]) + tail * carried


def key_kernel(heads, dk, cv, cum, slope, out):
    cols = jnp.transpose(cum[0])
    for i in range(heads):
        col = cols[:, i : i + 1]
        tail = jnp.exp(col[-1:, :] - col)
        total = dk[:, lanes(i)] + tail * cv[0, i : i + 1, :]
        out[:, lanes(i)] = (slope[:, lanes(i)].astype(F32) * total).astype(BF16)


def block_kernel(start, hops, quad, core, z, pattern, *refs):
    keep_out, send_out, adjoint_out, flags, lines, others = refs[-6:]
    pieces, (grads, parts), refs = refs[:QUAD], refs[QUAD : QUAD + 2], refs[QUAD + 2 : -7]
    reaches, other_pieces = refs[:hops], refs[hops:]
    tokens = grads.shape[1]
    key_rows = others.shape[1] - 8
    ncore = 1 + len(other_pieces)
    spike_rows = lines.shape[1] // ncore
    step = pl.program_id(0)
    tests = jnp.left_shift(1, 2 * lax.broadcasted_iota(jnp.int32, (8, tokens), 0))
    tests = [tests, 2 * tests]
    low = lax.broadcasted_iota(jnp.int32, (tokens, HEAD), 1) < BLK

    @pl.when(step == 0)
    def _():
        for i in range(QUAD):
            source = quad[0] ^ i
            others[source] = pieces[i][spike_rows:, :]
            for k in range(ncore):
                part = other_pieces[k - 1][i] if k else pieces[i][:spike_rows, :]
                rows = pl.multiple_of(lax.rem(core[0] + ncore - k, ncore) * spike_rows, spike_rows)
                lines[source, pl.ds(rows, spike_rows), :] = part.astype(jnp.int32)

    values = []
    for source in range(QUAD):
        reach = jnp.zeros((HEAD, HEAD), F32)
        for hop in range(hops):
            reach = jnp.where(z[0] == hops - 1 - hop, reaches[hop][source // 2, 0], reach)
        if source % 2:
            adjoint = reach
        else:
            adjoint = parts[source + 1, 0, :HEAD, :] + parts[source + 1, 0, HEAD : HEAD + 1, :] * reach
        adjoint_out[source, 0] = adjoint
        row = others[source, pl.ds(key_rows + start + step, 1), :]
        words = others[source, pl.ds(pl.multiple_of((start + step) * WORDS, WORDS), WORDS), :]
        k = unpack(words.astype(jnp.int32)) * jnp.exp(row[:, -1:] - row)
        carried = fold(tn(k.astype(BF16), jnp.concatenate(split(adjoint), axis=1)))
        values.append((grads[source] + carried).astype(BF16).astype(F32))
    for side in range(2):
        total = None
        for source in range(QUAD):
            grad = values[source]
            turned = jnp.concatenate([grad[:, BLK:], grad[:, :BLK]], axis=1)
            even, odd = (grad, turned) if side == 0 else (turned, grad)
            right = jnp.concatenate(
                [jnp.where(low, even, 0.0).astype(BF16), jnp.where(low, 0.0, odd).astype(BF16)], axis=0
            )
            for s in range(SEL):
                first = pattern[2 * (start + step) + side, s] * (BLK // 16)
                for parity in range(2):
                    flag_parts = []
                    for word in range(BLK // 16):
                        line = lines[source, pl.ds(first + word, 1), :]
                        spread = jnp.broadcast_to(line, (8, tokens))
                        spread = jnp.bitwise_and(spread, tests[parity])
                        flag_parts.append(jnp.where(spread != 0, 1.0, 0.0))
                    bits = jnp.concatenate(flag_parts, axis=0).astype(BF16)
                    flags[source, s * HALF : (s + 1) * HALF, parity * tokens : (parity + 1) * tokens] = bits
            part = nn(flags[source], right)
            total = part if total is None else total + part
        total = total.reshape(SEL, HALF, HEAD)
        keep_out[:, side] = total[: SEL // 2]
        send_out[:, side] = total[SEL // 2 :]


def finish_kernel(quad, *refs):
    parts, out = refs[:-1], refs[-1]
    rows = parts[0].shape[1]

    def place(source, offset):
        @pl.when(quad[0] ^ offset == source)
        def _():
            for n in range(CHUNKS):
                first = (source * CHUNKS + n) * rows
                for i in range(HALF):
                    out[0, first : first + rows, lanes(i)] = parts[n * QUAD + offset][0, :, i, :]

    for source in range(QUAD):
        for offset in range(QUAD):
            place(source, offset)


def per_device(
    input_spikes,
    query_spikes,
    key_spikes,
    values,
    query_slope,
    key_slope,
    grad_out,
    log_gate,
    pattern,
):
    tokens, width = values.shape
    heads_here = width // HEAD
    heads = heads_here // QUAD
    chunk = heads // CHUNKS
    nctx, ndp = lax.axis_size("ctx"), lax.axis_size("dp")
    nz = nctx // 2
    x, place = lax.axis_index("dp"), lax.axis_index("ctx")
    y, z = place % 2, place // 2
    quad = (2 * x + y).astype(jnp.int32).reshape(1)
    planes = [[d * nctx + 2 * c + i for d in range(ndp) for i in range(2)] for c in range(nz)]

    gate_sums = jnp.cumsum(log_gate, axis=1)
    cum = gate_sums.reshape(QUAD, heads, tokens)
    cum = jnp.pad(cum, ((0, 0), (0, 8 - heads), (0, 0)))

    def spec(block, index):
        return pl.BlockSpec(block, lambda j, *refs: index(j))

    word_spec = spec((heads * WORDS, tokens), lambda j: (j, 0))
    flat_spec = spec((tokens, heads * HEAD), lambda j: (0, j))
    cum_spec = spec((1, 8, tokens), lambda j: (j, 0, 0))
    vec_spec = spec((1, 8, HEAD), lambda j: (j, 0, 0))
    state_spec = spec((heads, HEAD, HEAD), lambda j: (j, 0, 0))
    wt_spec = spec((heads, tokens, tokens), lambda j: (j, 0, 0))
    col_spec = spec((1, tokens, 8), lambda j: (j, 0, 0))

    def shape(*dims, kind=F32):
        return jax.ShapeDtypeStruct(dims, kind)

    flat16 = shape(tokens, width, kind=BF16)
    flat32 = shape(tokens, width)
    states = shape(heads_here, HEAD, HEAD)
    vecs = shape(QUAD, 8, HEAD)
    cums = shape(QUAD, 8, tokens)
    unit = 2 * tokens * tokens * HEAD * heads_here
    mib = 1 << 20

    def call(name, kernel, in_specs, out_specs, out_shape, estimate, *args, scalars=0, aliases={}):
        def body(*refs):
            kernel(*refs)

        body.__name__ = name
        return pl.pallas_call(
            body,
            grid_spec=pltpu.PrefetchScalarGridSpec(
                num_scalar_prefetch=scalars, grid=(QUAD,), in_specs=in_specs, out_specs=out_specs
            ),
            out_shape=out_shape,
            input_output_aliases=aliases,
            compiler_params=params(),
            cost_estimate=estimate,
            name=name,
        )(*args)

    def swap(value):
        return lax.ppermute(value, "ctx", [(c, c ^ 1) for c in range(nctx)])

    def across(value, offset):
        pairs = [
            (d * nctx + c, (d ^ (offset // 2)) * nctx + (c ^ (offset % 2)))
            for d in range(ndp)
            for c in range(nctx)
        ]
        return lax.ppermute(value, ("dp", "ctx"), pairs)

    def plane(value):
        return lax.all_to_all(value, ("dp", "ctx"), 0, 0, axis_index_groups=planes, tiled=True)

    def ordered(own, got):
        return jnp.where(y == 0, own, got), jnp.where(y == 0, got, own)

    def carried_vectors(message, forward):
        parts = lax.all_to_all(message, "ctx", 0, 0, tiled=True)
        reach = jnp.zeros(vecs.shape, F32)
        for at in range(nctx) if forward else range(nctx - 1, -1, -1):
            inside = at < place if forward else at > place
            reach = jnp.where(inside, parts[at, :, 8:] * reach + parts[at, :, :8], reach)
        return reach, parts[:, :, 8 : 8 + heads, 0].reshape(nctx, heads_here)

    message_spec = spec((nctx, 1, 16, HEAD), lambda j: (0, j, 0, 0))
    messages = shape(nctx, QUAD, 16, HEAD)
    message = call(
        "key_sums_kernel",
        lambda *refs: key_sums_kernel(heads, *refs),
        [word_spec, cum_spec],
        message_spec,
        messages,
        cost(1, 1),
        key_spikes,
        cum,
    )
    z0, decays = carried_vectors(message, True)
    first_total = lax.dynamic_index_in_dim(decays, 2 * z, 0, keepdims=False)
    second_total = lax.dynamic_index_in_dim(decays, 2 * z + 1, 0, keepdims=False)

    ncore, core = lax.axis_size("tensor"), lax.axis_index("tensor")
    spike_rows = input_spikes.shape[0] // ncore
    spike_words = lax.dynamic_slice_in_dim(input_spikes, core * spike_rows, spike_rows, 0).astype(F32)
    spike_words = jnp.broadcast_to(spike_words[None], (QUAD,) + spike_words.shape)
    key_words = key_spikes.reshape(QUAD, heads * WORDS, tokens).astype(F32)
    key_words = jnp.concatenate([spike_words, key_words, cum], axis=1)
    pieces = []
    for i in range(QUAD):
        part = lax.dynamic_index_in_dim(key_words, quad[0] ^ i, 0, keepdims=False)
        pieces.append(across(part, i) if i else part)
    other_pieces = jnp.stack([piece[:spike_rows] for piece in pieces])
    other_pieces = [
        lax.ppermute(other_pieces, "tensor", [(c, (c + k) % ncore) for c in range(ncore)])
        for k in range(1, ncore)
    ]

    def state_half(side):
        return pl.pallas_call(
            lambda side, *refs: state_kernel(heads, *refs),
            grid_spec=pltpu.PrefetchScalarGridSpec(
                num_scalar_prefetch=1,
                grid=(2,),
                in_specs=[
                    pl.BlockSpec((heads * WORDS, tokens), lambda j, side: (2 * side[0] + j, 0)),
                    pl.BlockSpec((tokens, heads * HEAD), lambda j, side: (0, 2 * side[0] + j)),
                    pl.BlockSpec((1, 8, tokens), lambda j, side: (2 * side[0] + j, 0, 0)),
                ],
                out_specs=state_spec,
            ),
            out_shape=shape(heads_here // 2, HEAD, HEAD),
            compiler_params=params(),
            cost_estimate=cost(1, 1),
            name="state_kernel",
        )(side.astype(jnp.int32).reshape(1), key_spikes, values, cum)

    state_other = swap(state_half(1 - y))
    state_mine = state_half(y)
    wt, den_local, qt, kt = call(
        "weight_kernel",
        lambda *refs: weight_kernel(heads, *refs),
        [word_spec, word_spec, cum_spec],
        [wt_spec, cum_spec, flat_spec, flat_spec],
        [shape(heads_here, tokens, tokens, kind=BF16), cums, flat16, flat16],
        cost(1, 1),
        query_spikes,
        key_spikes,
        cum,
    )
    dens, adjoint_sums, value_parts = [], [], []
    anywhere = pl.BlockSpec(memory_space=pl.ANY)
    for n in range(CHUNKS):
        den, adjoint_sum, value_part = call(
            "adjoint_kernel",
            lambda *refs, n=n: adjoint_kernel(n * chunk, chunk, *refs),
            [
                spec((chunk * WORDS, tokens), lambda j, n=n: (j * CHUNKS + n, 0)),
                spec((tokens, chunk * HEAD), lambda j, n=n: (0, j * CHUNKS + n)),
                cum_spec,
                cum_spec,
                vec_spec,
                spec((chunk, tokens, tokens), lambda j, n=n: (j * CHUNKS + n, 0, 0)),
            ],
            [
                cum_spec,
                spec((1, chunk, HEAD + 8, HEAD), lambda j: (j, 0, 0, 0)),
                spec((1, tokens, chunk * HEAD), lambda j: (j, 0, 0)),
            ],
            [cums, shape(QUAD, chunk, HEAD + 8, HEAD), shape(QUAD, tokens, chunk * HEAD)],
            cost(1, 1),
            query_spikes,
            grad_out,
            cum,
            den_local,
            z0,
            wt,
        )
        dens.append(den)
        adjoint_sums.append(adjoint_sum)
        value_parts.append(value_part)

    local = call(
        "local_kernel",
        lambda wt, v, *refs: local_kernel(heads, wt, v, refs[-1]),
        [wt_spec, flat_spec] + [anywhere] * len([adjoint_sums[-1], *other_pieces]),
        flat_spec,
        flat32,
        cost(1, 1),
        wt,
        values,
        adjoint_sums[-1],
        *other_pieces,
    )

    half = heads_here // 2
    mine = y * half

    def cut(value, start):
        return lax.dynamic_slice_in_dim(value, start, half, 0)

    first, second = ordered(state_mine, state_other)
    first_decay = cut(first_total, mine)[:, None, None]
    second_decay = cut(second_total, mine)[:, None, None]
    state_both = second_decay * first + second
    state_decay = second_decay * first_decay
    part_size = half // CHUNKS

    at_z = z.astype(jnp.int32).reshape(1)
    hops, adjoint_parts = [], []
    for n in range(CHUNKS):
        received = plane(adjoint_sums[n])
        parts = received.reshape(2, 2, chunk, HEAD + 8, HEAD)
        gates = parts[:, :, :, HEAD : HEAD + 1, :1]
        down_decay = gates[:, 0] * gates[:, 1]
        size = (2, chunk, HEAD, HEAD)
        up = state_both[n * part_size : (n + 1) * part_size].reshape(size)
        size_spec = spec((1,) + size[1:], lambda j: (j, 0, 0, 0))
        down, send = pl.pallas_call(
            start_kernel,
            grid_spec=pltpu.PrefetchScalarGridSpec(
                num_scalar_prefetch=1,
                grid=(2,),
                in_specs=[
                    spec((2, chunk, HEAD + 8, HEAD), lambda j: (j, 0, 0, 0)),
                    size_spec,
                    anywhere,
                ],
                out_specs=[size_spec, size_spec],
            ),
            out_shape=[shape(*size), shape(*size)],
            compiler_params=params(),
            cost_estimate=cost(1, 1),
            name="start_kernel",
        )(at_z, received, up, local if n else received)
        up_decay = state_decay[n * part_size : (n + 1) * part_size].reshape(down_decay.shape)
        got = []
        for hop in range(nz - 1):
            if hop:
                send = jnp.where(z == hop, up, down) + jnp.where(z == hop, up_decay, down_decay) * got[-1]
            pairs = []
            for c in range(nctx):
                if c // 2 == hop:
                    pairs.append((c, c + 2))
                elif c // 2 == nz - 1 - hop:
                    pairs.append((c, c - 2))
            got.append(lax.ppermute(send, "ctx", pairs))
        hops.append(got)
        adjoint_parts.append(received)

    columns = pattern.shape[0] // QUAD
    share = SEL // nz
    own_pattern = lax.dynamic_slice_in_dim(pattern, quad[0] * columns, columns, 0)
    order = jnp.arange(nz, dtype=jnp.int32)
    turned = sum((order // (nz >> (bit + 1))) % 2 << bit for bit in range(nz.bit_length() - 1))
    order = ((z ^ turned)[:, None] * share + jnp.arange(share, dtype=jnp.int32)[None, :]).reshape(SEL)
    own_pattern = jnp.take(own_pattern, order, axis=1)
    columns = columns // CHUNKS
    terms_of, adjoints = [], []
    for n in range(CHUNKS):
        half_spec = spec((SEL // 2, 2, HALF, HEAD), lambda j: (0, j, 0, 0))
        half_shape = shape(SEL // 2, columns, HALF, HEAD)
        after = state_keep if n else adjoint_parts[n]
        summed, send, adjoint = pl.pallas_call(
            lambda *refs, n=n: block_kernel(n * chunk, nz - 1, *refs),
            grid_spec=pltpu.PrefetchScalarGridSpec(
                num_scalar_prefetch=4,
                grid=(chunk,),
                in_specs=[spec(piece.shape, lambda j: (0, 0)) for piece in pieces]
                + [
                    spec((QUAD, tokens, HEAD), lambda j: (0, 0, j)),
                    spec((QUAD, 1, HEAD + 8, HEAD), lambda j: (0, j, 0, 0)),
                ]
                + [spec((2, 1, HEAD, HEAD), lambda j: (0, j, 0, 0))] * (nz - 1)
                + [spec(piece.shape, lambda j: (0, 0, 0)) for piece in other_pieces]
                + [anywhere],
                out_specs=[half_spec, half_spec, spec((QUAD, 1, HEAD, HEAD), lambda j: (0, j, 0, 0))],
                scratch_shapes=[
                    pltpu.VMEM((QUAD, SEL * HALF, 2 * tokens), BF16),
                    pltpu.VMEM((QUAD, input_spikes.shape[0], tokens), jnp.int32),
                    pltpu.VMEM((QUAD, pieces[0].shape[0] - spike_rows, tokens), F32),
                ],
            ),
            out_shape=[half_shape, half_shape, shape(QUAD, chunk, HEAD, HEAD)],
            compiler_params=params(),
            cost_estimate=cost(1, 40 * mib),
            name="block_kernel",
        )(
            quad,
            core.astype(jnp.int32).reshape(1),
            at_z,
            own_pattern,
            *pieces,
            plane(value_parts[n]),
            adjoint_parts[n],
            *hops[n],
            *other_pieces,
            after,
        )
        adjoints.append(adjoint)

        terms = [summed]
        bit = 1
        while True:
            terms.append(lax.ppermute(send, "ctx", [(c, c ^ (2 * bit)) for c in range(nctx)]))
            bit *= 2
            if bit == nz:
                break
            rest = terms[0].shape[0] // 2
            send = sum(term[rest:] for term in terms)
            terms = [term[:rest] for term in terms]
        terms_of.append(terms)
        if n == 0:
            state_keep, state_send = pl.pallas_call(
                lambda *refs: turn_kernel([part_size] * CHUNKS, *refs),
                grid_spec=pltpu.PrefetchScalarGridSpec(
                    num_scalar_prefetch=2,
                    grid=(1,),
                    in_specs=[
                        spec((half, HEAD, HEAD), lambda j: (0, 0, 0)),
                        spec((half, 1, HEAD), lambda j: (0, 0, 0)),
                        anywhere,
                    ]
                    + [spec((part_size, HEAD, HEAD), lambda j: (0, 0, 0))] * (CHUNKS * (nz - 1)),
                    out_specs=[spec((half, HEAD, HEAD), lambda j: (0, 0, 0))] * 2,
                ),
                out_shape=[shape(half, HEAD, HEAD)] * 2,
                compiler_params=params(),
                cost_estimate=cost(1, 6 * mib),
                name="turn_kernel",
            )(
                at_z,
                y.astype(jnp.int32).reshape(1),
                first,
                jnp.broadcast_to(first_decay, (half, 1, HEAD)),
                adjoints[0],
                *[got.reshape(part_size, HEAD, HEAD) for n in range(CHUNKS) for got in hops[n]],
            )

    state = [y.astype(jnp.int32).reshape(1), state_keep, swap(state_send)]
    returned = [plane(adjoint) for adjoint in adjoints]
    part_spec = spec((heads, HEAD, HEAD), lambda j: (j % 2, 0, 0))
    h, xv = call(
        "output_kernel",
        lambda *refs: output_kernel(chunk, heads, *refs),
        [part_spec] * 2 + [flat_spec] * 3 + [cum_spec] * (1 + CHUNKS) + [anywhere],
        [col_spec, message_spec],
        [shape(QUAD, tokens, 8), messages],
        cost(1, 40 * mib),
        *state,
        local,
        qt,
        grad_out,
        cum,
        *dens,
        returned[0],
        scalars=1,
    )
    cv = carried_vectors(xv, False)[0]
    dq, dk = call(
        "token_kernel",
        lambda *refs: token_kernel(chunk, heads, *refs),
        [part_spec, part_spec, vec_spec]
        + [flat_spec] * 4
        + [cum_spec, flat_spec, col_spec]
        + [cum_spec] * CHUNKS
        + [spec((1, chunk, HEAD, HEAD), lambda j: (j, 0, 0, 0))] * CHUNKS,
        [flat_spec, flat_spec],
        [flat16, flat32],
        cost(1, 60 * mib),
        *state,
        z0,
        qt,
        kt,
        values,
        grad_out,
        cum,
        query_slope,
        h,
        *dens,
        *returned,
        scalars=1,
    )
    results = []
    for n in range(CHUNKS):
        order = dq if n == CHUNKS - 1 else adjoints[-1]
        half_spec = pl.BlockSpec((share // 2, columns, HALF, HEAD), lambda j, y: (y[0], 0, 0, 0))
        other_spec = pl.BlockSpec((share // 2, columns, HALF, HEAD), lambda j, y: (1 - y[0], 0, 0, 0))
        part_shape = shape(share // 2, columns, HALF, HEAD)
        whole_spec = pl.BlockSpec(part_shape.shape, lambda j, y: (0, 0, 0, 0))
        own, other = pl.pallas_call(
            sum_kernel,
            grid_spec=pltpu.PrefetchScalarGridSpec(
                num_scalar_prefetch=1,
                grid=(1,),
                in_specs=[half_spec, other_spec] * len(terms_of[n]) + [anywhere],
                out_specs=[whole_spec, whole_spec],
            ),
            out_shape=[part_shape, part_shape],
            compiler_params=params(),
            cost_estimate=cost(1, 4 * mib),
            name="sum_kernel",
        )(y.astype(jnp.int32).reshape(1), *[term for term in terms_of[n] for _ in range(2)], order)
        results += [own, across(other, 1), across(own, 2), across(other, 3)]
    part_spec = spec((1, columns, HALF, HEAD), lambda j: (j, 0, 0, 0))
    value_grad = pl.pallas_call(
        finish_kernel,
        grid_spec=pltpu.PrefetchScalarGridSpec(
            num_scalar_prefetch=1,
            grid=(share // 2,),
            in_specs=[part_spec] * (CHUNKS * QUAD),
            out_specs=spec((1, pattern.shape[0], BLK * BLK), lambda j: (j, 0, 0)),
        ),
        out_shape=shape(share // 2, pattern.shape[0], BLK * BLK),
        compiler_params=params(),
        cost_estimate=cost(1, 4 * mib),
        name="finish_kernel",
    )(quad, *results)

    key_grad = call(
        "key_kernel",
        lambda *refs: key_kernel(heads, *refs),
        [flat_spec, vec_spec, cum_spec, flat_spec],
        flat_spec,
        flat16,
        cost(1, 8 * mib),
        dk,
        cv,
        cum,
        key_slope,
    )
    return (dq, key_grad, value_grad)


def solution(mesh):
    in_specs = (
        P(None, ("dp", "ctx")),
        P("tensor", ("dp", "ctx")),
        P("tensor", ("dp", "ctx")),
        P(("dp", "ctx"), "tensor"),
        P(("dp", "ctx"), "tensor"),
        P(("dp", "ctx"), "tensor"),
        P(("dp", "ctx"), "tensor"),
        P("tensor", ("dp", "ctx")),
        P("tensor", None),
    )
    out_specs = (P(("dp", "ctx"), "tensor"), P(("dp", "ctx"), "tensor"), P("ctx", "tensor", None))
    return jax.shard_map(
        per_device, mesh=mesh, in_specs=in_specs, out_specs=out_specs, check_vma=False
    )
```

```python
import jax
import jax.numpy as jnp
from jax import lax
from jax.experimental import pallas as pl
from jax.experimental.pallas import tpu as pltpu
from jax.sharding import PartitionSpec as P

HEAD = 128
WORDS = HEAD // 16
BLK = 64
HALF = BLK // 2
SEL = 16
QUAD = 4
CHUNKS = 2

F32 = jnp.float32
BF16 = jnp.bfloat16
VMEM_LIMIT = 62 * 1024 * 1024


def params():
    return pltpu.CompilerParams(vmem_limit_bytes=VMEM_LIMIT)


def cost(flops, nbytes):
    return pl.CostEstimate(flops=int(flops), bytes_accessed=int(nbytes), transcendentals=0)


def nn(a, b):
    return lax.dot_general(a, b, (((1,), (0,)), ((), ())), preferred_element_type=F32)


def nt(a, b):
    return lax.dot_general(a, b, (((1,), (1,)), ((), ())), preferred_element_type=F32)


def tn(a, b):
    return lax.dot_general(a, b, (((0,), (0,)), ((), ())), preferred_element_type=F32)


def split(a):
    high = a.astype(BF16)
    return high, (a - high.astype(F32)).astype(BF16)


def fold(a):
    return a[:, :HEAD] + a[:, HEAD:]


def unpack(words):
    tokens = words.shape[1]
    spread = jnp.broadcast_to(words[:, None, :], (WORDS, 16, tokens))
    shifts = lax.broadcasted_iota(jnp.int32, (WORDS, 16, tokens), 1)
    bits = jnp.bitwise_and(jnp.right_shift(spread, shifts), 1)
    return bits.reshape(HEAD, tokens).astype(F32)


def causal(shape, token_axis):
    return lax.broadcasted_iota(jnp.int32, shape, token_axis) >= lax.broadcasted_iota(
        jnp.int32, shape, 1 - token_axis
    )


def lanes(i):
    return slice(i * HEAD, (i + 1) * HEAD)


def rows_of(vector):
    high, low = split(vector)
    low2 = (vector - high.astype(F32) - low.astype(F32)).astype(BF16)
    n = vector.shape[1]
    return jnp.concatenate([high, low, low2, jnp.zeros((13, n), BF16)], axis=0)


def put_message(out, i, vector, total):
    copies = out.shape[0]
    out[:, 0, i : i + 1, :] = jnp.broadcast_to(vector[None], (copies, 1, HEAD))
    out[:, 0, 8 + i : 9 + i, :] = jnp.broadcast_to(total[None], (copies, 1, HEAD))


def key_sums_kernel(heads, kw, cum, out):
    for i in range(heads):
        row = cum[0, i : i + 1, :]
        tail = jnp.exp(row[:, -1:] - row)
        k = unpack(kw[i * WORDS : (i + 1) * WORDS, :]).astype(BF16)
        vector = jnp.sum(nt(rows_of(tail), k), axis=0, keepdims=True)
        put_message(out, i, vector, jnp.exp(row[:, -1:]))


def state_kernel(heads, kw, v, cum, y_out):
    for i in range(heads):
        row = cum[0, i : i + 1, :]
        k = unpack(kw[i * WORDS : (i + 1) * WORDS, :])
        high, low = split(k * jnp.exp(row[:, -1:] - row))
        value = v[:, lanes(i)]
        y_out[i] = nn(high, value) + nn(low, value)


def weight_kernel(heads, qw, kw, cum, wt_out, den_out, qt_out, kt_out):
    tokens = kt_out.shape[0]
    cols = jnp.transpose(cum[0])
    after = causal((tokens, tokens), 1)
    for i in range(heads):
        row = cum[0, i : i + 1, :]
        col = cols[:, i : i + 1]
        q = unpack(qw[i * WORDS : (i + 1) * WORDS, :])
        kt = jnp.transpose(unpack(kw[i * WORDS : (i + 1) * WORDS, :])).astype(BF16)
        kt_out[:, lanes(i)] = kt
        qt_out[:, lanes(i)] = jnp.transpose(q).astype(BF16)
        decay = jnp.where(after, jnp.exp(jnp.minimum(row - col, 0.0)), 0.0)
        w = nn(kt, q.astype(BF16)) * decay
        wt_out[i] = w.astype(BF16)
        den_out[0, i : i + 1, :] = jnp.sum(w, axis=0, keepdims=True)


def start_kernel(z, received, up, order, down_out, send_out):
    second = received[1, :, :HEAD, :]
    down = received[0, :, :HEAD, :] + received[0, :, HEAD : HEAD + 1, :] * second
    down_out[0] = down
    send_out[0] = jnp.where(z[0] == 0, up[0], down)


def turn_kernel(sizes, z, y, first, decay, order, *refs):
    hops, (keep_out, send_out) = refs[:-2], refs[-2:]
    count = len(hops) // CHUNKS
    for n in range(CHUNKS):
        for i in range(sizes[n]):
            at = n * sizes[0] + i
            reach = jnp.zeros((HEAD, HEAD), F32)
            for hop in range(count):
                reach = jnp.where(z[0] == hop + 1, hops[n * count + hop][i], reach)
            later = decay[at] * reach + first[at]
            keep_out[at] = jnp.where(y[0] == 0, reach, later)
            send_out[at] = jnp.where(y[0] == 0, later, reach)


def half_kernel(*refs):
    terms, out = refs[:-2], refs[-1]
    out[...] = sum((term[...] for term in terms[1:]), terms[0][...])


def sum_kernel(y, *refs):
    terms, (own_out, other_out) = refs[:-3], refs[-2:]
    own_out[...] = sum((term[...] for term in terms[2::2]), terms[0][...])
    other_out[...] = sum((term[...] for term in terms[3::2]), terms[1][...])


def local_kernel(heads, wt, v, out):
    for i in range(heads):
        out[:, lanes(i)] = tn(wt[i], v[:, lanes(i)])


def adjoint_kernel(start, heads, qw, do, cum, den_local, z0, wt, den_out, x_out, dv_out):
    tokens = do.shape[0]
    rows = []
    qs = []
    for i in range(heads):
        at = start + i
        row = cum[0, at : at + 1, :]
        q = unpack(qw[i * WORDS : (i + 1) * WORDS, :]).astype(BF16)
        qs.append(q)
        carried = jnp.sum(nn(rows_of(z0[0, at : at + 1, :]), q), axis=0, keepdims=True)
        rows.append(1.0 + den_local[0, at : at + 1, :] + jnp.exp(row) * carried)
    rows = rows + [jnp.ones((1, tokens), F32)] * (8 - heads)
    den = jnp.concatenate(rows, axis=0)
    den_out[0] = den
    inverse = jnp.transpose(1.0 / den)
    leads = jnp.exp(jnp.transpose(cum[0]))
    for i in range(heads):
        g = do[:, lanes(i)].astype(F32) * inverse[:, i : i + 1]
        lead = leads[:, start + i : start + i + 1]
        x_out[0, i, :HEAD, :] = fold(nn(qs[i], jnp.concatenate(split(g * lead), axis=1)))
        x_out[0, i, HEAD:, :] = jnp.broadcast_to(lead[-1:, :], (8, HEAD))
        dv_out[0, :, lanes(i)] = nn(wt[i], g.astype(BF16))


def output_kernel(chunk, heads, y, keep, got, local, qt, do, cum, *refs):
    dens, (h_out, xv_out) = refs[:CHUNKS], refs[-2:]
    cols = jnp.transpose(cum[0])
    inverses = [jnp.transpose(1.0 / den[0]) for den in dens]
    kept = pl.program_id(0) // 2 == y[0]
    for i in range(heads):
        col = cols[:, i : i + 1]
        inverse = inverses[i // chunk][:, i % chunk : i % chunk + 1]
        lead = jnp.exp(col)
        q = qt[:, lanes(i)]
        grad = do[:, lanes(i)].astype(F32)
        state = jnp.where(kept, keep[i], got[i])
        carried = fold(nn(q, jnp.concatenate(split(state), axis=1)))
        o = (local[:, lanes(i)] + lead * carried) * inverse
        h = -jnp.sum(grad * o, axis=1, keepdims=True) * inverse
        h_out[0, :, i : i + 1] = h
        vector = jnp.sum(q.astype(F32) * (lead * h), axis=0, keepdims=True)
        put_message(xv_out, i, vector, lead[-1:, :])


def token_kernel(chunk, heads, y, keep, got, z0, qt, kt, v, do, cum, slope, h_in, *refs):
    dens, adjoints, (dq_out, dk_out) = refs[:CHUNKS], refs[CHUNKS:-2], refs[-2:]
    tokens = v.shape[0]
    cols = jnp.transpose(cum[0])
    inverses = [jnp.transpose(1.0 / den[0]) for den in dens]
    before = causal((tokens, tokens), 0)
    kept = pl.program_id(0) // 2 == y[0]
    for i in range(heads):
        row = cum[0, i : i + 1, :]
        col = cols[:, i : i + 1]
        inverse = inverses[i // chunk][:, i % chunk : i % chunk + 1]
        lead = jnp.exp(col)
        tail = jnp.exp(col[-1:, :] - col)
        value = v[:, lanes(i)]
        decay = jnp.where(before, jnp.exp(jnp.minimum(col - row, 0.0)), 0.0)
        h = h_in[0, :, i : i + 1]
        g = (do[:, lanes(i)].astype(F32) * inverse).astype(BF16)
        r = ((nt(g, value) + h) * decay).astype(BF16)
        state = jnp.where(kept, keep[i], got[i])
        back = fold(nt(g, jnp.concatenate(split(state), axis=0))) + h * z0[0, i : i + 1, :]
        dq = nn(r, kt[:, lanes(i)]) + lead * back
        dq_out[:, lanes(i)] = (slope[:, lanes(i)].astype(F32) * dq).astype(BF16)
        adjoint = adjoints[i // chunk][0, i % chunk]
        carried = fold(nt(value, jnp.concatenate(split(adjoint), axis=0)))
        dk_out[:, lanes(i)] = tn(r, qt[:, lanes(i)]) + tail * carried


def key_kernel(heads, dk, cv, cum, slope, out):
    cols = jnp.transpose(cum[0])
    for i in range(heads):
        col = cols[:, i : i + 1]
        tail = jnp.exp(col[-1:, :] - col)
        total = dk[:, lanes(i)] + tail * cv[0, i : i + 1, :]
        out[:, lanes(i)] = (slope[:, lanes(i)].astype(F32) * total).astype(BF16)


def block_kernel(start, hops, quad, core, z, pattern, *refs):
    keep_out, send_out, adjoint_out, flags, lines, others = refs[-6:]
    pieces, (grads, parts), refs = refs[:QUAD], refs[QUAD : QUAD + 2], refs[QUAD + 2 : -7]
    reaches, other_pieces = refs[:hops], refs[hops:]
    tokens = grads.shape[1]
    key_rows = others.shape[1] - 8
    ncore = 1 + len(other_pieces)
    spike_rows = lines.shape[1] // ncore
    step = pl.program_id(0)
    tests = jnp.left_shift(1, 2 * lax.broadcasted_iota(jnp.int32, (8, tokens), 0))
    tests = [tests, 2 * tests]
    low = lax.broadcasted_iota(jnp.int32, (tokens, HEAD), 1) < BLK

    @pl.when(step == 0)
    def _():
        for i in range(QUAD):
            source = quad[0] ^ i
            others[source] = pieces[i][spike_rows:, :]
            for k in range(ncore):
                part = other_pieces[k - 1][i] if k else pieces[i][:spike_rows, :]
                rows = pl.multiple_of(lax.rem(core[0] + ncore - k, ncore) * spike_rows, spike_rows)
                lines[source, pl.ds(rows, spike_rows), :] = part.astype(jnp.int32)

    values = []
    for source in range(QUAD):
        reach = jnp.zeros((HEAD, HEAD), F32)
        for hop in range(hops):
            reach = jnp.where(z[0] == hops - 1 - hop, reaches[hop][source // 2, 0], reach)
        if source % 2:
            adjoint = reach
        else:
            adjoint = parts[source + 1, 0, :HEAD, :] + parts[source + 1, 0, HEAD : HEAD + 1, :] * reach
        adjoint_out[source, 0] = adjoint
        row = others[source, pl.ds(key_rows + start + step, 1), :]
        words = others[source, pl.ds(pl.multiple_of((start + step) * WORDS, WORDS), WORDS), :]
        k = unpack(words.astype(jnp.int32)) * jnp.exp(row[:, -1:] - row)
        carried = fold(tn(k.astype(BF16), jnp.concatenate(split(adjoint), axis=1)))
        values.append((grads[source] + carried).astype(BF16).astype(F32))
    for side in range(2):
        total = None
        for source in range(QUAD):
            grad = values[source]
            turned = jnp.concatenate([grad[:, BLK:], grad[:, :BLK]], axis=1)
            even, odd = (grad, turned) if side == 0 else (turned, grad)
            right = jnp.concatenate(
                [jnp.where(low, even, 0.0).astype(BF16), jnp.where(low, 0.0, odd).astype(BF16)], axis=0
            )
            for s in range(SEL):
                first = pattern[2 * (start + step) + side, s] * (BLK // 16)
                for parity in range(2):
                    flag_parts = []
                    for word in range(BLK // 16):
                        line = lines[source, pl.ds(first + word, 1), :]
                        spread = jnp.broadcast_to(line, (8, tokens))
                        spread = jnp.bitwise_and(spread, tests[parity])
                        flag_parts.append(jnp.where(spread != 0, 1.0, 0.0))
                    bits = jnp.concatenate(flag_parts, axis=0).astype(BF16)
                    flags[source, s * HALF : (s + 1) * HALF, parity * tokens : (parity + 1) * tokens] = bits
            part = nn(flags[source], right)
            total = part if total is None else total + part
        total = total.reshape(SEL, HALF, HEAD)
        keep_out[:, side] = total[: SEL // 2]
        send_out[:, side] = total[SEL // 2 :]


def finish_kernel(quad, *refs):
    parts, out = refs[:-1], refs[-1]
    rows = parts[0].shape[1]

    def place(source, offset):
        @pl.when(quad[0] ^ offset == source)
        def _():
            for n in range(CHUNKS):
                first = (source * CHUNKS + n) * rows
                for i in range(HALF):
                    out[0, first : first + rows, lanes(i)] = parts[n * QUAD + offset][0, :, i, :]

    for source in range(QUAD):
        for offset in range(QUAD):
            place(source, offset)


def per_device(
    input_spikes,
    query_spikes,
    key_spikes,
    values,
    query_slope,
    key_slope,
    grad_out,
    log_gate,
    pattern,
):
    tokens, width = values.shape
    heads_here = width // HEAD
    heads = heads_here // QUAD
    chunk = heads // CHUNKS
    nctx, ndp = lax.axis_size("ctx"), lax.axis_size("dp")
    nz = nctx // 2
    x, place = lax.axis_index("dp"), lax.axis_index("ctx")
    y, z = place % 2, place // 2
    quad = (2 * x + y).astype(jnp.int32).reshape(1)
    planes = [[d * nctx + 2 * c + i for d in range(ndp) for i in range(2)] for c in range(nz)]

    gate_sums = jnp.cumsum(log_gate, axis=1)
    cum = gate_sums.reshape(QUAD, heads, tokens)
    cum = jnp.pad(cum, ((0, 0), (0, 8 - heads), (0, 0)))

    def spec(block, index):
        return pl.BlockSpec(block, lambda j, *refs: index(j))

    word_spec = spec((heads * WORDS, tokens), lambda j: (j, 0))
    flat_spec = spec((tokens, heads * HEAD), lambda j: (0, j))
    cum_spec = spec((1, 8, tokens), lambda j: (j, 0, 0))
    vec_spec = spec((1, 8, HEAD), lambda j: (j, 0, 0))
    state_spec = spec((heads, HEAD, HEAD), lambda j: (j, 0, 0))
    wt_spec = spec((heads, tokens, tokens), lambda j: (j, 0, 0))
    col_spec = spec((1, tokens, 8), lambda j: (j, 0, 0))

    def shape(*dims, kind=F32):
        return jax.ShapeDtypeStruct(dims, kind)

    flat16 = shape(tokens, width, kind=BF16)
    flat32 = shape(tokens, width)
    states = shape(heads_here, HEAD, HEAD)
    vecs = shape(QUAD, 8, HEAD)
    cums = shape(QUAD, 8, tokens)
    unit = 2 * tokens * tokens * HEAD * heads_here
    mib = 1 << 20

    def call(name, kernel, in_specs, out_specs, out_shape, estimate, *args, scalars=0, aliases={}):
        def body(*refs):
            kernel(*refs)

        body.__name__ = name
        return pl.pallas_call(
            body,
            grid_spec=pltpu.PrefetchScalarGridSpec(
                num_scalar_prefetch=scalars, grid=(QUAD,), in_specs=in_specs, out_specs=out_specs
            ),
            out_shape=out_shape,
            input_output_aliases=aliases,
            compiler_params=params(),
            cost_estimate=estimate,
            name=name,
        )(*args)

    def swap(value):
        return lax.ppermute(value, "ctx", [(c, c ^ 1) for c in range(nctx)])

    def across(value, offset):
        pairs = [
            (d * nctx + c, (d ^ (offset // 2)) * nctx + (c ^ (offset % 2)))
            for d in range(ndp)
            for c in range(nctx)
        ]
        return lax.ppermute(value, ("dp", "ctx"), pairs)

    def plane(value):
        return lax.all_to_all(value, ("dp", "ctx"), 0, 0, axis_index_groups=planes, tiled=True)

    def ordered(own, got):
        return jnp.where(y == 0, own, got), jnp.where(y == 0, got, own)

    def carried_vectors(message, forward):
        parts = lax.all_to_all(message, "ctx", 0, 0, tiled=True)
        reach = jnp.zeros(vecs.shape, F32)
        for at in range(nctx) if forward else range(nctx - 1, -1, -1):
            inside = at < place if forward else at > place
            reach = jnp.where(inside, parts[at, :, 8:] * reach + parts[at, :, :8], reach)
        return reach, parts[:, :, 8 : 8 + heads, 0].reshape(nctx, heads_here)

    message_spec = spec((nctx, 1, 16, HEAD), lambda j: (0, j, 0, 0))
    messages = shape(nctx, QUAD, 16, HEAD)
    message = call(
        "key_sums_kernel",
        lambda *refs: key_sums_kernel(heads, *refs),
        [word_spec, cum_spec],
        message_spec,
        messages,
        cost(1, 1),
        key_spikes,
        cum,
    )
    z0, decays = carried_vectors(message, True)
    first_total = lax.dynamic_index_in_dim(decays, 2 * z, 0, keepdims=False)
    second_total = lax.dynamic_index_in_dim(decays, 2 * z + 1, 0, keepdims=False)

    ncore, core = lax.axis_size("tensor"), lax.axis_index("tensor")
    spike_rows = input_spikes.shape[0] // ncore
    spike_words = lax.dynamic_slice_in_dim(input_spikes, core * spike_rows, spike_rows, 0).astype(F32)
    spike_words = jnp.broadcast_to(spike_words[None], (QUAD,) + spike_words.shape)
    key_words = key_spikes.reshape(QUAD, heads * WORDS, tokens).astype(F32)
    key_words = jnp.concatenate([spike_words, key_words, cum], axis=1)
    pieces = []
    for i in range(QUAD):
        part = lax.dynamic_index_in_dim(key_words, quad[0] ^ i, 0, keepdims=False)
        pieces.append(across(part, i) if i else part)
    other_pieces = jnp.stack([piece[:spike_rows] for piece in pieces])
    other_pieces = [
        lax.ppermute(other_pieces, "tensor", [(c, (c + k) % ncore) for c in range(ncore)])
        for k in range(1, ncore)
    ]

    def state_half(side):
        return pl.pallas_call(
            lambda side, *refs: state_kernel(heads, *refs),
            grid_spec=pltpu.PrefetchScalarGridSpec(
                num_scalar_prefetch=1,
                grid=(2,),
                in_specs=[
                    pl.BlockSpec((heads * WORDS, tokens), lambda j, side: (2 * side[0] + j, 0)),
                    pl.BlockSpec((tokens, heads * HEAD), lambda j, side: (0, 2 * side[0] + j)),
                    pl.BlockSpec((1, 8, tokens), lambda j, side: (2 * side[0] + j, 0, 0)),
                ],
                out_specs=state_spec,
            ),
            out_shape=shape(heads_here // 2, HEAD, HEAD),
            compiler_params=params(),
            cost_estimate=cost(1, 1),
            name="state_kernel",
        )(side.astype(jnp.int32).reshape(1), key_spikes, values, cum)

    state_other = swap(state_half(1 - y))
    state_mine = state_half(y)
    wt, den_local, qt, kt = call(
        "weight_kernel",
        lambda *refs: weight_kernel(heads, *refs),
        [word_spec, word_spec, cum_spec],
        [wt_spec, cum_spec, flat_spec, flat_spec],
        [shape(heads_here, tokens, tokens, kind=BF16), cums, flat16, flat16],
        cost(1, 1),
        query_spikes,
        key_spikes,
        cum,
    )
    dens, adjoint_sums, value_parts = [], [], []
    anywhere = pl.BlockSpec(memory_space=pl.ANY)
    for n in range(CHUNKS):
        den, adjoint_sum, value_part = call(
            "adjoint_kernel",
            lambda *refs, n=n: adjoint_kernel(n * chunk, chunk, *refs),
            [
                spec((chunk * WORDS, tokens), lambda j, n=n: (j * CHUNKS + n, 0)),
                spec((tokens, chunk * HEAD), lambda j, n=n: (0, j * CHUNKS + n)),
                cum_spec,
                cum_spec,
                vec_spec,
                spec((chunk, tokens, tokens), lambda j, n=n: (j * CHUNKS + n, 0, 0)),
            ],
            [
                cum_spec,
                spec((1, chunk, HEAD + 8, HEAD), lambda j: (j, 0, 0, 0)),
                spec((1, tokens, chunk * HEAD), lambda j: (j, 0, 0)),
            ],
            [cums, shape(QUAD, chunk, HEAD + 8, HEAD), shape(QUAD, tokens, chunk * HEAD)],
            cost(1, 1),
            query_spikes,
            grad_out,
            cum,
            den_local,
            z0,
            wt,
        )
        dens.append(den)
        adjoint_sums.append(adjoint_sum)
        value_parts.append(value_part)

    local = call(
        "local_kernel",
        lambda wt, v, *refs: local_kernel(heads, wt, v, refs[-1]),
        [wt_spec, flat_spec] + [anywhere] * len([adjoint_sums[-1], *other_pieces]),
        flat_spec,
        flat32,
        cost(1, 1),
        wt,
        values,
        adjoint_sums[-1],
        *other_pieces,
    )

    half = heads_here // 2
    mine = y * half

    def cut(value, start):
        return lax.dynamic_slice_in_dim(value, start, half, 0)

    first, second = ordered(state_mine, state_other)
    first_decay = cut(first_total, mine)[:, None, None]
    second_decay = cut(second_total, mine)[:, None, None]
    state_both = second_decay * first + second
    state_decay = second_decay * first_decay
    part_size = half // CHUNKS

    at_z = z.astype(jnp.int32).reshape(1)
    hops, adjoint_parts = [], []
    for n in range(CHUNKS):
        received = plane(adjoint_sums[n])
        parts = received.reshape(2, 2, chunk, HEAD + 8, HEAD)
        gates = parts[:, :, :, HEAD : HEAD + 1, :1]
        down_decay = gates[:, 0] * gates[:, 1]
        size = (2, chunk, HEAD, HEAD)
        up = state_both[n * part_size : (n + 1) * part_size].reshape(size)
        size_spec = spec((1,) + size[1:], lambda j: (j, 0, 0, 0))
        down, send = pl.pallas_call(
            start_kernel,
            grid_spec=pltpu.PrefetchScalarGridSpec(
                num_scalar_prefetch=1,
                grid=(2,),
                in_specs=[
                    spec((2, chunk, HEAD + 8, HEAD), lambda j: (j, 0, 0, 0)),
                    size_spec,
                    anywhere,
                ],
                out_specs=[size_spec, size_spec],
            ),
            out_shape=[shape(*size), shape(*size)],
            compiler_params=params(),
            cost_estimate=cost(1, 1),
            name="start_kernel",
        )(at_z, received, up, local if n else received)
        up_decay = state_decay[n * part_size : (n + 1) * part_size].reshape(down_decay.shape)
        got = []
        for hop in range(nz - 1):
            if hop:
                send = jnp.where(z == hop, up, down) + jnp.where(z == hop, up_decay, down_decay) * got[-1]
            pairs = []
            for c in range(nctx):
                if c // 2 == hop:
                    pairs.append((c, c + 2))
                elif c // 2 == nz - 1 - hop:
                    pairs.append((c, c - 2))
            got.append(lax.ppermute(send, "ctx", pairs))
        hops.append(got)
        adjoint_parts.append(received)

    columns = pattern.shape[0] // QUAD
    share = SEL // nz
    own_pattern = lax.dynamic_slice_in_dim(pattern, quad[0] * columns, columns, 0)
    order = jnp.arange(nz, dtype=jnp.int32)
    turned = sum((order // (nz >> (bit + 1))) % 2 << bit for bit in range(nz.bit_length() - 1))
    order = ((z ^ turned)[:, None] * share + jnp.arange(share, dtype=jnp.int32)[None, :]).reshape(SEL)
    own_pattern = jnp.take(own_pattern, order, axis=1)
    columns = columns // CHUNKS
    terms_of, adjoints = [], []
    for n in range(CHUNKS):
        half_spec = spec((SEL // 2, 2, HALF, HEAD), lambda j: (0, j, 0, 0))
        half_shape = shape(SEL // 2, columns, HALF, HEAD)
        after = state_keep if n else adjoint_parts[n]
        summed, send, adjoint = pl.pallas_call(
            lambda *refs, n=n: block_kernel(n * chunk, nz - 1, *refs),
            grid_spec=pltpu.PrefetchScalarGridSpec(
                num_scalar_prefetch=4,
                grid=(chunk,),
                in_specs=[spec(piece.shape, lambda j: (0, 0)) for piece in pieces]
                + [
                    spec((QUAD, tokens, HEAD), lambda j: (0, 0, j)),
                    spec((QUAD, 1, HEAD + 8, HEAD), lambda j: (0, j, 0, 0)),
                ]
                + [spec((2, 1, HEAD, HEAD), lambda j: (0, j, 0, 0))] * (nz - 1)
                + [spec(piece.shape, lambda j: (0, 0, 0)) for piece in other_pieces]
                + [anywhere],
                out_specs=[half_spec, half_spec, spec((QUAD, 1, HEAD, HEAD), lambda j: (0, j, 0, 0))],
                scratch_shapes=[
                    pltpu.VMEM((QUAD, SEL * HALF, 2 * tokens), BF16),
                    pltpu.VMEM((QUAD, input_spikes.shape[0], tokens), jnp.int32),
                    pltpu.VMEM((QUAD, pieces[0].shape[0] - spike_rows, tokens), F32),
                ],
            ),
            out_shape=[half_shape, half_shape, shape(QUAD, chunk, HEAD, HEAD)],
            compiler_params=params(),
            cost_estimate=cost(1, 40 * mib),
            name="block_kernel",
        )(
            quad,
            core.astype(jnp.int32).reshape(1),
            at_z,
            own_pattern,
            *pieces,
            plane(value_parts[n]),
            adjoint_parts[n],
            *hops[n],
            *other_pieces,
            after,
        )
        adjoints.append(adjoint)

        terms = [summed]
        terms.append(lax.ppermute(send, "ctx", [(c, c ^ 2) for c in range(nctx)]))
        terms_of.append(terms)
        if n == 0:
            state_keep, state_send = pl.pallas_call(
                lambda *refs: turn_kernel([part_size] * CHUNKS, *refs),
                grid_spec=pltpu.PrefetchScalarGridSpec(
                    num_scalar_prefetch=2,
                    grid=(1,),
                    in_specs=[
                        spec((half, HEAD, HEAD), lambda j: (0, 0, 0)),
                        spec((half, 1, HEAD), lambda j: (0, 0, 0)),
                        anywhere,
                    ]
                    + [spec((part_size, HEAD, HEAD), lambda j: (0, 0, 0))] * (CHUNKS * (nz - 1)),
                    out_specs=[spec((half, HEAD, HEAD), lambda j: (0, 0, 0))] * 2,
                ),
                out_shape=[shape(half, HEAD, HEAD)] * 2,
                compiler_params=params(),
                cost_estimate=cost(1, 6 * mib),
                name="turn_kernel",
            )(
                at_z,
                y.astype(jnp.int32).reshape(1),
                first,
                jnp.broadcast_to(first_decay, (half, 1, HEAD)),
                adjoints[0],
                *[got.reshape(part_size, HEAD, HEAD) for n in range(CHUNKS) for got in hops[n]],
            )

    state = [y.astype(jnp.int32).reshape(1), state_keep, swap(state_send)]
    returned = [plane(adjoint) for adjoint in adjoints]
    part_spec = spec((heads, HEAD, HEAD), lambda j: (j % 2, 0, 0))
    h, xv = call(
        "output_kernel",
        lambda *refs: output_kernel(chunk, heads, *refs),
        [part_spec] * 2 + [flat_spec] * 3 + [cum_spec] * (1 + CHUNKS) + [anywhere],
        [col_spec, message_spec],
        [shape(QUAD, tokens, 8), messages],
        cost(1, 40 * mib),
        *state,
        local,
        qt,
        grad_out,
        cum,
        *dens,
        returned[0],
        scalars=1,
    )
    bit, rest, order = 2, SEL // 4, terms_of[1][0]
    while bit < nz:
        for n in range(CHUNKS):
            part_shape = (rest, columns, HALF, HEAD)
            send = pl.pallas_call(
                half_kernel,
                grid=(1,),
                in_specs=[spec(part_shape, lambda j: (1, 0, 0, 0))] * len(terms_of[n]) + [anywhere],
                out_specs=spec(part_shape, lambda j: (0, 0, 0, 0)),
                out_shape=shape(*part_shape),
                compiler_params=params(),
                cost_estimate=cost(1, 1),
                name="half_kernel",
            )(*terms_of[n], order)
            order = h
            terms_of[n].append(
                lax.ppermute(send, "ctx", [(c, c ^ (2 * bit)) for c in range(nctx)])
            )
        bit *= 2
        rest //= 2
    cv = carried_vectors(xv, False)[0]
    dq, dk = call(
        "token_kernel",
        lambda *refs: token_kernel(chunk, heads, *refs),
        [part_spec, part_spec, vec_spec]
        + [flat_spec] * 4
        + [cum_spec, flat_spec, col_spec]
        + [cum_spec] * CHUNKS
        + [spec((1, chunk, HEAD, HEAD), lambda j: (j, 0, 0, 0))] * CHUNKS,
        [flat_spec, flat_spec],
        [flat16, flat32],
        cost(1, 60 * mib),
        *state,
        z0,
        qt,
        kt,
        values,
        grad_out,
        cum,
        query_slope,
        h,
        *dens,
        *returned,
        scalars=1,
    )
    results = []
    for n in range(CHUNKS):
        order = dq if n == CHUNKS - 1 else adjoints[-1]
        half_spec = pl.BlockSpec((share // 2, columns, HALF, HEAD), lambda j, y: (y[0], 0, 0, 0))
        other_spec = pl.BlockSpec((share // 2, columns, HALF, HEAD), lambda j, y: (1 - y[0], 0, 0, 0))
        part_shape = shape(share // 2, columns, HALF, HEAD)
        whole_spec = pl.BlockSpec(part_shape.shape, lambda j, y: (0, 0, 0, 0))
        own, other = pl.pallas_call(
            sum_kernel,
            grid_spec=pltpu.PrefetchScalarGridSpec(
                num_scalar_prefetch=1,
                grid=(1,),
                in_specs=[half_spec, other_spec] * len(terms_of[n]) + [anywhere],
                out_specs=[whole_spec, whole_spec],
            ),
            out_shape=[part_shape, part_shape],
            compiler_params=params(),
            cost_estimate=cost(1, 4 * mib),
            name="sum_kernel",
        )(y.astype(jnp.int32).reshape(1), *[term for term in terms_of[n] for _ in range(2)], order)
        results += [own, across(other, 1), across(own, 2), across(other, 3)]
    part_spec = spec((1, columns, HALF, HEAD), lambda j: (j, 0, 0, 0))
    value_grad = pl.pallas_call(
        finish_kernel,
        grid_spec=pltpu.PrefetchScalarGridSpec(
            num_scalar_prefetch=1,
            grid=(share // 2,),
            in_specs=[part_spec] * (CHUNKS * QUAD),
            out_specs=spec((1, pattern.shape[0], BLK * BLK), lambda j: (j, 0, 0)),
        ),
        out_shape=shape(share // 2, pattern.shape[0], BLK * BLK),
        compiler_params=params(),
        cost_estimate=cost(1, 4 * mib),
        name="finish_kernel",
    )(quad, *results)

    key_grad = call(
        "key_kernel",
        lambda *refs: key_kernel(heads, *refs),
        [flat_spec, vec_spec, cum_spec, flat_spec],
        flat_spec,
        flat16,
        cost(1, 8 * mib),
        dk,
        cv,
        cum,
        key_slope,
    )
    return (dq, key_grad, value_grad)


def solution(mesh):
    in_specs = (
        P(None, ("dp", "ctx")),
        P("tensor", ("dp", "ctx")),
        P("tensor", ("dp", "ctx")),
        P(("dp", "ctx"), "tensor"),
        P(("dp", "ctx"), "tensor"),
        P(("dp", "ctx"), "tensor"),
        P(("dp", "ctx"), "tensor"),
        P("tensor", ("dp", "ctx")),
        P("tensor", None),
    )
    out_specs = (P(("dp", "ctx"), "tensor"), P(("dp", "ctx"), "tensor"), P("ctx", "tensor", None))
    return jax.shard_map(
        per_device, mesh=mesh, in_specs=in_specs, out_specs=out_specs, check_vma=False
    )
```
